256 devices in a mesh: seq: 32 (over y, z), tp: 8 (over x, core).
Axes of the slice: x: 4, y: 4, z: 8, core: 2. Of those that a mesh axis runs over, the one named last changes fastest.
Arguments:
- queries: bfloat16 [12288, 5120], P('seq', 'tp'), may hold values from -8 to 8
- key_rows: bfloat16 [12288, 5120], P('seq', 'tp'), may hold values from -8 to 8
- values: bfloat16 [12288, 5120], P('seq', 'tp'), may hold values from -6 to 6
- out_weight: bfloat16 [5120, 5120], P('tp', 'seq'), may hold values from -0.3125 to 0.3125
- grad_out: bfloat16 [12288, 5120], P('seq', 'tp'), may hold values from -1.5 to 1.5
- labels: int32 [12288], P('seq'), may hold values from 0 to 127, as said below
- owner_map: int32 [128], replicated, may hold values from 0 to 31, as said below
- pair_mask: int32 [128, 128], replicated, may hold values from 0 to 1, as said below
Outputs:
- output: bfloat16 [12288, 5120], P('seq', 'tp')
- grad_queries: bfloat16 [12288, 5120], P('seq', 'tp')
- grad_keys: bfloat16 [12288, 5120], P('seq', 'tp')
- grad_values: bfloat16 [12288, 5120], P('seq', 'tp')
The draws below stay inside these ranges and needn't reach their ends.
Inputs may be any that keep to these rules, and one draw needn't show every extreme that they name: `labels`: of the 384 tokens of one index of seq, at most 24 lie in clusters of any one owner; in every draw some owner receives exactly 24 from every index, 768 in all. `owner_map`: every owner index holds exactly 4 clusters. pair_mask[a, b] is 1 only where owner_map[a] == owner_map[b], and pair_mask[a, a] = 1.
All inputs are finite; a program needn't handle non-finite values.
Results may differ from the reference program's by a relative error of at most 0.017.
Values may be sent and summed in bfloat16 or wider, within the bound.
No kernel may reach another device: no remote copies, remote signals or barrier semaphores. Data moves between devices by JAX's collectives and lax.ppermute only.
A program may use at most 64 MiB of HBM per device.

```python
import jax
import jax.numpy as jnp
from jax import lax

D = 5120
HEADS = 40
HEAD = 128
TOK_DEV = 384
CL_DEV = 4
TOKENS = 12288
CLUSTERS = 128
SLOT = 24
CAP = 768
GROUP = 640
N_SEQ = 32
N_TP = 8


def cluster_plan(key):
    shuffle = jax.random.permutation(jax.random.fold_in(key, 101), CLUSTERS).astype(jnp.int32)
    owners = shuffle // CL_DEV
    members = jnp.argsort(shuffle).astype(jnp.int32)
    return (owners, members)


def draw_owner_map(key, part):
    owners, members = cluster_plan(key)
    return owners.astype(jnp.int32)


def draw_pair_mask(key, part):
    owners, members = cluster_plan(key)
    key = jax.random.fold_in(key, 3)
    coin_flips = jax.random.randint(key, (CLUSTERS, CLUSTERS), 0, 2).astype(jnp.int32)
    same_owner = owners[:, None] == owners[None, :]
    cluster_ids = jnp.arange(CLUSTERS, dtype=jnp.int32)
    diagonal = cluster_ids[:, None] == cluster_ids[None, :]
    return jnp.where(diagonal, 1, jnp.where(same_owner, coin_flips, 0)).astype(jnp.int32)


def device_labels(device_key, busiest, members):
    quarter = N_SEQ // 4
    rest_count = N_SEQ - quarter
    half_rows = TOK_DEV // 2
    owner_ids = jnp.arange(N_SEQ, dtype=jnp.int32)
    priority = jax.random.permutation(jax.random.fold_in(device_key, 1), N_SEQ).astype(jnp.int32)
    priority = jnp.where(owner_ids == busiest, -1, priority)
    ranked = jnp.argsort(priority).astype(jnp.int32)
    weights = jax.random.randint(jax.random.fold_in(device_key, 2), (rest_count,), 1, 3).astype(jnp.int32)
    bounds = (half_rows * jnp.cumsum(weights) // jnp.sum(weights)).astype(jnp.int32)
    rest_counts = bounds - jnp.concatenate([jnp.zeros((1,), jnp.int32), bounds[:-1]])
    per_owner = jnp.zeros((N_SEQ,), jnp.int32).at[ranked[:quarter]].set(SLOT).at[ranked[quarter:]].set(rest_counts)
    owner_edges = jnp.cumsum(per_owner).astype(jnp.int32)
    positions = jnp.arange(TOK_DEV, dtype=jnp.int32)
    target = jnp.sum((positions[:, None] >= owner_edges[None, :]).astype(jnp.int32), axis=1)
    member_rank = jax.random.randint(jax.random.fold_in(device_key, 3), (TOK_DEV,), 0, CL_DEV).astype(jnp.int32)
    chosen = members[target * CL_DEV + member_rank]
    return chosen[jax.random.permutation(jax.random.fold_in(device_key, 4), TOK_DEV)]


def draw_labels(key, part):
    owners, members = cluster_plan(key)
    key = jax.random.fold_in(key, 5)
    busiest = jax.random.randint(jax.random.fold_in(key, 0), (), 0, N_SEQ).astype(jnp.int32)
    device_keys = jax.random.split(jax.random.fold_in(key, 1), N_SEQ)
    all_rows = jax.vmap(lambda device_key: device_labels(device_key, busiest, members))(device_keys)
    return all_rows.reshape(TOKENS).astype(jnp.int32)


def draw_queries(key, part):
    key = jax.random.fold_in(key, 11)
    return jnp.clip(jax.random.normal(key, (TOKENS, D), jnp.float32), -8.0, 8.0).astype(jnp.bfloat16)


def draw_key_rows(key, part):
    key = jax.random.fold_in(key, 13)
    return jnp.clip(jax.random.normal(key, (TOKENS, D), jnp.float32), -8.0, 8.0).astype(jnp.bfloat16)


def shard_levels(rng, extent, cuts, low, top_value):
    gain, own = 1.0, jax.random.fold_in(rng, 6)
    for position, blocks in cuts:
        draws = jnp.exp(jax.random.uniform(jax.random.fold_in(own, position), (blocks,), jnp.float32, low / len(cuts), top_value / len(cuts)))
        gain = gain * jnp.repeat(draws, extent[position] // blocks).reshape([-1 if axis == position else 1 for axis in range(len(extent))])
    return gain


def noise(key, extent, scale, limit, shards=(), kind=jnp.bfloat16):
    entries = jax.random.normal(key, extent, jnp.float32) * scale
    if len(shards) > 0:
        entries = shard_levels(key, extent, shards, -0.22, 0.18) * entries
    return jnp.clip(entries, min=-limit, max=limit).astype(kind)


def setup_inputs(seed: int = 0) -> dict:
    arg_keys = jax.random.split(jax.random.key(seed), 9)
    return {
        "queries": draw_queries(jax.random.fold_in(arg_keys[8], 71), 0),
        "key_rows": draw_key_rows(jax.random.fold_in(arg_keys[8], 71), 0),
        "values": noise(arg_keys[2], (TOKENS, D), 1.0, 6.0, ((0, 32), (1, 8))),
        "out_weight": noise(arg_keys[3], (D, D), (D // 16) ** -0.5, 0.3125, ((0, 8), (1, 32))),
        "grad_out": noise(arg_keys[4], (TOKENS, D), 0.25, 1.5, ((0, 32), (1, 8))),
        "labels": draw_labels(jax.random.fold_in(arg_keys[8], 71), 0),
        "owner_map": draw_owner_map(jax.random.fold_in(arg_keys[8], 71), 0),
        "pair_mask": draw_pair_mask(jax.random.fold_in(arg_keys[8], 71), 0),
    }


NEG_FILL = -1e30


def head_weights(query_head, key_head, allowed, head_scale):
    scores = jnp.dot(query_head, key_head.T, preferred_element_type=jnp.float32) * head_scale
    scores = jnp.where(allowed, scores, NEG_FILL)
    row_top = jnp.max(scores, axis=1, keepdims=True)
    exp_terms = jnp.exp(scores - row_top)
    return exp_terms / jnp.sum(exp_terms, axis=1, keepdims=True)


def head_forward(query_head, key_head, value_head, allowed, head_scale):
    weights = head_weights(query_head, key_head, allowed, head_scale)
    return jnp.dot(weights.astype(jnp.bfloat16), value_head, preferred_element_type=jnp.float32).astype(jnp.bfloat16)


def head_backward(query_head, key_head, value_head, attended, grad_att, allowed, head_scale):
    weights = head_weights(query_head, key_head, allowed, head_scale)
    weights_low = weights.astype(jnp.bfloat16)
    grad_probs = jnp.dot(grad_att, value_head.T, preferred_element_type=jnp.float32)
    delta_rows = jnp.sum(grad_att.astype(jnp.float32) * attended.astype(jnp.float32), axis=1, keepdims=True)
    grad_scores = (weights * (grad_probs - delta_rows)).astype(jnp.bfloat16)
    grad_query = (jnp.dot(grad_scores, key_head, preferred_element_type=jnp.float32) * head_scale).astype(jnp.bfloat16)
    grad_key = (jnp.dot(grad_scores.T, query_head, preferred_element_type=jnp.float32) * head_scale).astype(jnp.bfloat16)
    grad_value = jnp.dot(weights_low.T, grad_att, preferred_element_type=jnp.float32).astype(jnp.bfloat16)
    return grad_query, grad_key, grad_value


def split_heads(matrix):
    return jnp.transpose(matrix.reshape(matrix.shape[0], HEADS, HEAD), (1, 0, 2))


def join_heads(stacked):
    return jnp.transpose(stacked, (1, 0, 2)).reshape(stacked.shape[1], -1)


def reference(queries, key_rows, values, out_weight, grad_out, labels, owner_map, pair_mask):
    head_scale = HEAD ** -0.5
    grad_att = jnp.dot(grad_out, out_weight.T, preferred_element_type=jnp.float32).astype(jnp.bfloat16)
    token_owner = owner_map[labels]
    sort_order = jnp.argsort(token_owner, stable=True).astype(jnp.int32)
    owner_ids = jnp.arange(N_SEQ, dtype=jnp.int32)
    counts = jnp.sum((token_owner[None, :] == owner_ids[:, None]).astype(jnp.int32), axis=1)
    starts = (jnp.cumsum(counts) - counts).astype(jnp.int32)

    def sort_pad(matrix):
        return jnp.concatenate([matrix[sort_order], jnp.zeros((CAP,) + matrix.shape[1:], matrix.dtype)], axis=0)

    sorted_q = sort_pad(queries)
    sorted_k = sort_pad(key_rows)
    sorted_v = sort_pad(values)
    sorted_g = sort_pad(grad_att)
    sorted_labels = sort_pad(labels)
    empty_rows = jnp.zeros((TOKENS + CAP, D), jnp.bfloat16)

    def one_owner(owner_index, results):
        first_row = starts[owner_index]
        valid_rows = jnp.arange(CAP, dtype=jnp.int32) < counts[owner_index]

        def window(matrix):
            return lax.dynamic_slice_in_dim(matrix, first_row, CAP, 0)

        group_labels = window(sorted_labels)
        allowed = (pair_mask[group_labels][:, group_labels] == 1) & valid_rows[:, None] & valid_rows[None, :]
        group_grad = jnp.where(valid_rows[:, None], window(sorted_g), jnp.zeros((), jnp.bfloat16))
        heads_q = split_heads(window(sorted_q))
        heads_k = split_heads(window(sorted_k))
        heads_v = split_heads(window(sorted_v))
        attended = lax.map(lambda pieces: head_forward(pieces[0], pieces[1], pieces[2], allowed, head_scale), (heads_q, heads_k, heads_v))
        grad_heads = lax.map(lambda pieces: head_backward(pieces[0], pieces[1], pieces[2], pieces[3], pieces[4], allowed, head_scale), (heads_q, heads_k, heads_v, attended, split_heads(group_grad)))
        updated = (attended, grad_heads[0], grad_heads[1], grad_heads[2])
        return tuple(lax.dynamic_update_slice_in_dim(current, join_heads(fresh_rows), first_row, 0) for current, fresh_rows in zip(results, updated))

    results = lax.fori_loop(0, N_SEQ, one_owner, (empty_rows, empty_rows, empty_rows, empty_rows))
    inverse = jnp.zeros((TOKENS,), jnp.int32).at[sort_order].set(jnp.arange(TOKENS, dtype=jnp.int32))
    attended_all, grad_q_all, grad_k_all, grad_v_all = [current[:TOKENS][inverse] for current in results]
    output = jnp.zeros((TOKENS, D), jnp.float32)
    for group_index in range(N_TP):
        columns = slice(group_index * GROUP, (group_index + 1) * GROUP)
        group_part = jnp.dot(attended_all[:, columns], out_weight[columns, :], preferred_element_type=jnp.float32).astype(jnp.bfloat16)
        output = output + group_part.astype(jnp.float32)
    return (output.astype(jnp.bfloat16), grad_q_all, grad_k_all, grad_v_all)
```

```python
import jax
import jax.numpy as jnp
from jax import lax
from jax.experimental import pallas as pl
from jax.experimental.pallas import tpu as pltpu
from jax.sharding import PartitionSpec as P

HEAD = 128
NEG_FILL = -1e30
VMEM_BYTES = 48 * 1024 * 1024
NT = (((1,), (1,)), ((), ()))


def dot32(left, right):
    return jnp.dot(left, right, preferred_element_type=jnp.float32)


def dot32_nt(left, right):
    return lax.dot_general(left, right, NT, preferred_element_type=jnp.float32)


def params():
    return pltpu.CompilerParams(vmem_limit_bytes=VMEM_BYTES)


def pack_kernel(seq_count, slot_size, label_row, label_col, owner_col, q_ref, k_ref, v_ref, packed, dest_row, dest_col):
    rows = q_ref.shape[0]
    cols = q_ref.shape[1]
    clusters = owner_col.shape[0]
    buffer_rows = packed.shape[0]
    in_cluster = label_row[...] == lax.broadcasted_iota(jnp.int32, (clusters, rows), 0)
    owner_row = jnp.sum(jnp.where(in_cluster, owner_col[...], 0), axis=0, keepdims=True)
    owned = owner_row == lax.broadcasted_iota(jnp.int32, (seq_count, rows), 0)
    earlier = lax.broadcasted_iota(jnp.int32, (rows, rows), 0) < lax.broadcasted_iota(
        jnp.int32, (rows, rows), 1
    )
    before = dot32(
        owned.astype(jnp.float32).astype(jnp.bfloat16), earlier.astype(jnp.float32).astype(jnp.bfloat16)
    )
    rank_row = jnp.sum(jnp.where(owned, before, 0.0), axis=0, keepdims=True)
    dest = owner_row * slot_size + rank_row.astype(jnp.int32)
    dest_row[...] = dest
    wide = jnp.broadcast_to(dest.astype(jnp.float32), (HEAD, rows))
    dest_col[...] = jnp.transpose(wide).astype(jnp.int32)
    select = (lax.broadcasted_iota(jnp.int32, (buffer_rows, rows), 0) == dest).astype(jnp.float32).astype(jnp.bfloat16)
    packed[:, 0:cols] = dot32(select, q_ref[...]).astype(jnp.bfloat16)
    packed[:, cols : 2 * cols] = dot32(select, k_ref[...]).astype(jnp.bfloat16)
    packed[:, 2 * cols : 3 * cols] = dot32(select, v_ref[...]).astype(jnp.bfloat16)
    codes = jnp.broadcast_to((label_col[...] + 1).astype(jnp.float32), (rows, HEAD)).astype(jnp.bfloat16)
    packed[:, 3 * cols :] = dot32(select, codes).astype(jnp.bfloat16)


def pack_inputs(seq_count, slot_size, labels, owner_map, queries, key_rows, values):
    rows, cols = queries.shape
    buffer_rows = seq_count * slot_size
    return pl.pallas_call(
        lambda *refs: pack_kernel(seq_count, slot_size, *refs),
        out_shape=(
            jax.ShapeDtypeStruct((buffer_rows, 3 * cols + HEAD), jnp.bfloat16),
            jax.ShapeDtypeStruct((1, rows), jnp.int32),
            jax.ShapeDtypeStruct((rows, HEAD), jnp.int32),
        ),
        compiler_params=params(),
    )(labels[None, :], labels[:, None], owner_map[:, None], queries, key_rows, values)


def forward_kernel(scale, chunk, q_ref, k_ref, v_ref, code_ref, mask_ref, att_ref, weight_ref, bias):
    rows = q_ref.shape[0]

    @pl.when(pl.program_id(0) == 0)
    def _():
        lane = lax.broadcasted_iota(jnp.int32, (rows, HEAD), 1).astype(jnp.float32) + 1.0
        onehot = (code_ref[...].astype(jnp.float32) == lane).astype(jnp.float32).astype(jnp.bfloat16)
        linked = dot32(onehot, mask_ref[...]).astype(jnp.bfloat16)
        for start in range(0, rows, chunk):
            linked_part = linked[start : start + chunk]
            allowed = dot32_nt(onehot, linked_part) > 0.5
            bias[:, start : start + chunk] = jnp.where(allowed, 0.0, NEG_FILL)

    value_t = jnp.transpose(v_ref[...])
    for start in range(0, rows, chunk):
        part = slice(start, start + chunk)
        scores = dot32_nt(k_ref[...], q_ref[part, :]) * scale + bias[:, part]
        top = jnp.max(scores, axis=0, keepdims=True)
        terms = jnp.exp(scores - top)
        weights = (terms * (1.0 / jnp.sum(terms, axis=0, keepdims=True))).astype(jnp.bfloat16)
        weight_ref[0, :, part] = weights
        att_ref[part, :] = jnp.transpose(dot32(value_t, weights)).astype(jnp.bfloat16)


def backward_kernel(scale, chunk, q_ref, k_ref, v_ref, att_ref, g_ref, weight_ref, out_ref):
    rows = q_ref.shape[0]
    grad = g_ref[...]
    delta = jnp.sum(
        jnp.transpose(grad.astype(jnp.float32) * att_ref[...].astype(jnp.float32)), axis=0, keepdims=True
    )
    key_t = jnp.transpose(k_ref[...])
    grad_key = jnp.zeros((rows, HEAD), jnp.float32)
    grad_value = jnp.zeros((rows, HEAD), jnp.float32)
    for start in range(0, rows, chunk):
        part = slice(start, start + chunk)
        weights = weight_ref[0, :, part]
        grad_part = g_ref[part, :]
        grad_probs = dot32_nt(v_ref[...], grad_part)
        grad_scores = (weights.astype(jnp.float32) * (grad_probs - delta[:, part])).astype(jnp.bfloat16)
        out_ref[part, 0:HEAD] = jnp.transpose(dot32(key_t, grad_scores) * scale).astype(jnp.bfloat16)
        grad_key = grad_key + dot32(grad_scores, q_ref[part, :])
        grad_value = grad_value + dot32(weights, grad_part)
    out_ref[:, HEAD : 2 * HEAD] = (grad_key * scale).astype(jnp.bfloat16)
    out_ref[:, 2 * HEAD :] = grad_value.astype(jnp.bfloat16)


def attention_forward(owned, pair_mask, heads, scale, chunk):
    rows = owned.shape[0]
    block = (rows, HEAD)
    return pl.pallas_call(
        lambda *refs: forward_kernel(scale, chunk, *refs),
        grid=(heads,),
        in_specs=[
            pl.BlockSpec(block, lambda h: (0, h)),
            pl.BlockSpec(block, lambda h: (0, heads + h)),
            pl.BlockSpec(block, lambda h: (0, 2 * heads + h)),
            pl.BlockSpec(block, lambda h: (0, 3 * heads)),
            pl.BlockSpec(pair_mask.shape, lambda h: (0, 0)),
        ],
        out_specs=(
            pl.BlockSpec(block, lambda h: (0, h)),
            pl.BlockSpec((1, rows, rows), lambda h: (h, 0, 0)),
        ),
        out_shape=(
            jax.ShapeDtypeStruct((rows, heads * HEAD), jnp.bfloat16),
            jax.ShapeDtypeStruct((heads, rows, rows), jnp.bfloat16),
        ),
        scratch_shapes=[pltpu.VMEM((rows, rows), jnp.float32)],
        compiler_params=params(),
        cost_estimate=pl.CostEstimate(
            flops=heads * 4 * rows * rows * HEAD,
            bytes_accessed=heads * rows * (8 * HEAD + 2 * rows),
            transcendentals=heads * rows * rows,
        ),
    )(owned, owned, owned, owned, pair_mask)


def attention_backward(owned, attended, grad_owned, weights, heads, scale, chunk):
    rows = owned.shape[0]
    block = (rows, HEAD)
    return pl.pallas_call(
        lambda *refs: backward_kernel(scale, chunk, *refs),
        grid=(heads,),
        in_specs=[
            pl.BlockSpec(block, lambda h: (0, h)),
            pl.BlockSpec(block, lambda h: (0, heads + h)),
            pl.BlockSpec(block, lambda h: (0, 2 * heads + h)),
            pl.BlockSpec(block, lambda h: (0, h)),
            pl.BlockSpec(block, lambda h: (0, h)),
            pl.BlockSpec((1, rows, rows), lambda h: (h, 0, 0)),
        ],
        out_specs=pl.BlockSpec((rows, 3 * HEAD), lambda h: (0, h)),
        out_shape=jax.ShapeDtypeStruct((rows, 3 * heads * HEAD), jnp.bfloat16),
        compiler_params=params(),
        cost_estimate=pl.CostEstimate(
            flops=heads * 8 * rows * rows * HEAD,
            bytes_accessed=heads * rows * (16 * HEAD + 2 * rows),
            transcendentals=0,
        ),
    )(owned, owned, owned, attended, grad_owned, weights)


def unpack_kernel(dest_ref, blocks_ref, q_ref, k_ref, v_ref):
    rows = q_ref.shape[0]
    buffer_rows = blocks_ref.shape[0]
    select = (
        dest_ref[:, 0:1] == lax.broadcasted_iota(jnp.int32, (rows, buffer_rows), 1)
    ).astype(jnp.float32).astype(jnp.bfloat16)
    for place, out_ref in enumerate((q_ref, k_ref, v_ref)):
        part = blocks_ref[:, place * HEAD : (place + 1) * HEAD]
        out_ref[...] = dot32(select, part).astype(jnp.bfloat16)


def unpack_grads(dest_col, blocks, heads):
    rows = dest_col.shape[0]
    buffer_rows = blocks.shape[0]
    out = jax.ShapeDtypeStruct((rows, heads * HEAD), jnp.bfloat16)
    return pl.pallas_call(
        unpack_kernel,
        grid=(heads,),
        in_specs=[
            pl.BlockSpec((rows, HEAD), lambda h: (0, 0)),
            pl.BlockSpec((buffer_rows, 3 * HEAD), lambda h: (0, h)),
        ],
        out_specs=[pl.BlockSpec((rows, HEAD), lambda h: (0, h))] * 3,
        out_shape=(out, out, out),
        compiler_params=params(),
        cost_estimate=pl.CostEstimate(
            flops=6 * heads * rows * buffer_rows * HEAD,
            bytes_accessed=6 * heads * HEAD * (rows + buffer_rows),
            transcendentals=0,
        ),
    )(dest_col, blocks)


def exchange(matrix, seq_count):
    rows, cols = matrix.shape
    blocks = matrix.reshape(seq_count, rows // seq_count, cols)
    return lax.all_to_all(blocks, "seq", split_axis=0, concat_axis=0, tiled=True).reshape(rows, cols)


def body(queries, key_rows, values, out_weight, grad_out, labels, owner_map, pair_mask):
    seq_count = lax.axis_size("seq")
    row_count, width = queries.shape
    heads = width // HEAD
    slot_size = 2 * row_count // seq_count
    buffer_rows = seq_count * slot_size
    scale = HEAD ** (-0.5)
    chunk = 256
    full_weight = lax.all_gather(out_weight, "seq", axis=1, tiled=True)
    grad_full = lax.all_gather(grad_out, "tp", axis=1, tiled=True)
    packed, dest_row, dest_col = pack_inputs(
        seq_count, slot_size, labels, owner_map, queries, key_rows, values
    )
    owned = exchange(packed, seq_count)
    attended, weights = attention_forward(owned, pair_mask.astype(jnp.bfloat16), heads, scale, chunk)
    returned = exchange(attended, seq_count)
    grad_att = lax.dot_general(grad_full, full_weight, NT, preferred_element_type=jnp.float32).astype(
        jnp.bfloat16
    )
    place = jnp.arange(buffer_rows, dtype=jnp.int32)
    grad_packed = dot32((place[:, None] == dest_row).astype(jnp.bfloat16), grad_att).astype(jnp.bfloat16)
    grad_owned = exchange(grad_packed, seq_count)
    attended_local = dot32((dest_col[:, 0:1] == place[None, :]).astype(jnp.bfloat16), returned).astype(
        jnp.bfloat16
    )
    partial_out = dot32(attended_local, full_weight).astype(jnp.bfloat16)
    output = lax.psum_scatter(partial_out, "tp", scatter_dimension=1, tiled=True)
    grads = attention_backward(owned, attended, grad_owned, weights, heads, scale, chunk)
    back = exchange(grads, seq_count)
    grad_q, grad_k, grad_v = unpack_grads(dest_col, back, heads)
    return (output, grad_q, grad_k, grad_v)


def solution(mesh):
    in_specs = (
        P("seq", "tp"),
        P("seq", "tp"),
        P("seq", "tp"),
        P("tp", "seq"),
        P("seq", "tp"),
        P("seq"),
        P(),
        P(),
    )
    out_specs = (P("seq", "tp"), P("seq", "tp"), P("seq", "tp"), P("seq", "tp"))
    return jax.shard_map(body, mesh=mesh, in_specs=in_specs, out_specs=out_specs, check_vma=False)
```

```python
import jax
import jax.numpy as jnp
from jax import lax
from jax.experimental import pallas as pl
from jax.experimental.pallas import tpu as pltpu
from jax.sharding import PartitionSpec as P

HEAD = 128
NEG_FILL = -1e30
VMEM_BYTES = 48 * 1024 * 1024
NT = (((1,), (1,)), ((), ()))


def dot32(left, right):
    return jnp.dot(left, right, preferred_element_type=jnp.float32)


def dot32_nt(left, right):
    return lax.dot_general(left, right, NT, preferred_element_type=jnp.float32)


def params():
    return pltpu.CompilerParams(vmem_limit_bytes=VMEM_BYTES)


def as_bf16(flags):
    return flags.astype(jnp.float32).astype(jnp.bfloat16)


def column_of(row):
    wide = jnp.broadcast_to(row.astype(jnp.float32), (HEAD, row.shape[1]))
    return jnp.transpose(wide)


def pack_kernel(seq_count, slot_size, label_row, owner_row_ref, q_ref, k_ref, v_ref, packed, dest_row, dest_col):
    rows, cols = q_ref.shape
    clusters = owner_row_ref.shape[1]
    buffer_rows = packed.shape[0]
    labels = label_row[...]
    owner_col = column_of(owner_row_ref[...])[:, 0:1].astype(jnp.int32)
    in_cluster = labels == lax.broadcasted_iota(jnp.int32, (clusters, rows), 0)
    owner_row = jnp.sum(jnp.where(in_cluster, owner_col, 0), axis=0, keepdims=True)
    owned = owner_row == lax.broadcasted_iota(jnp.int32, (seq_count, rows), 0)
    earlier = lax.broadcasted_iota(jnp.int32, (rows, rows), 0) < lax.broadcasted_iota(
        jnp.int32, (rows, rows), 1
    )
    before = dot32(as_bf16(owned), as_bf16(earlier))
    rank_row = jnp.sum(jnp.where(owned, before, 0.0), axis=0, keepdims=True)
    dest = owner_row * slot_size + rank_row.astype(jnp.int32)
    dest_row[...] = dest
    dest_col[...] = column_of(dest).astype(jnp.int32)
    select = as_bf16(lax.broadcasted_iota(jnp.int32, (buffer_rows, rows), 0) == dest)
    packed[:, 0:cols] = dot32(select, q_ref[...]).astype(jnp.bfloat16)
    packed[:, cols : 2 * cols] = dot32(select, k_ref[...]).astype(jnp.bfloat16)
    packed[:, 2 * cols : 3 * cols] = dot32(select, v_ref[...]).astype(jnp.bfloat16)
    packed[:, 3 * cols :] = dot32(select, column_of(labels + 1).astype(jnp.bfloat16)).astype(jnp.bfloat16)


def pack_inputs(seq_count, slot_size, labels, owner_map, queries, key_rows, values):
    rows, cols = queries.shape
    buffer_rows = seq_count * slot_size
    return pl.pallas_call(
        lambda *refs: pack_kernel(seq_count, slot_size, *refs),
        out_shape=(
            jax.ShapeDtypeStruct((buffer_rows, 3 * cols + HEAD), jnp.bfloat16),
            jax.ShapeDtypeStruct((1, rows), jnp.int32),
            jax.ShapeDtypeStruct((rows, HEAD), jnp.int32),
        ),
        compiler_params=params(),
    )(labels[None, :], owner_map[None, :], queries, key_rows, values)


def grad_kernel(order_ref, grad_ref, weight_ref, dest_row, packed, total):
    step = pl.program_id(0)

    @pl.when(step == 0)
    def _():
        total[...] = jnp.zeros_like(total)

    total[...] += dot32(grad_ref[0], weight_ref[...])

    @pl.when(step == pl.num_programs(0) - 1)
    def _():
        select = as_bf16(lax.broadcasted_iota(jnp.int32, (packed.shape[0], total.shape[0]), 0) == dest_row[...])
        packed[...] = dot32(select, total[...].astype(jnp.bfloat16)).astype(jnp.bfloat16)


def project_grads(order, grad_blocks, weight_t, dest_row, buffer_rows):
    groups, rows, width = grad_blocks.shape
    return pl.pallas_call(
        grad_kernel,
        grid_spec=pltpu.PrefetchScalarGridSpec(
            num_scalar_prefetch=1,
            grid=(groups,),
            in_specs=[
                pl.BlockSpec((1, rows, width), lambda g, order: (g, 0, 0)),
                pl.BlockSpec((width, width), lambda g, order: (order[g], 0)),
                pl.BlockSpec((1, rows), lambda g, order: (0, 0)),
            ],
            out_specs=pl.BlockSpec((buffer_rows, width), lambda g, order: (0, 0)),
            scratch_shapes=[pltpu.VMEM((rows, width), jnp.float32)],
        ),
        out_shape=jax.ShapeDtypeStruct((buffer_rows, width), jnp.bfloat16),
        compiler_params=params(),
        cost_estimate=pl.CostEstimate(
            flops=2 * groups * rows * width * width + 2 * buffer_rows * rows * width,
            bytes_accessed=2 * groups * width * (rows + width),
            transcendentals=0,
        ),
    )(order, grad_blocks, weight_t, dest_row)


def output_kernel(dest_col, returned, weight_ref, out_ref, local):
    @pl.when(pl.program_id(0) == 0)
    def _():
        place = lax.broadcasted_iota(jnp.int32, (local.shape[0], returned.shape[0]), 1)
        local[...] = dot32(as_bf16(dest_col[:, 0:1] == place), returned[...]).astype(jnp.bfloat16)

    out_ref[0] = dot32_nt(local[...], weight_ref[...]).astype(jnp.bfloat16)


def project_output(dest_col, returned, weight_t, groups):
    rows = dest_col.shape[0]
    buffer_rows, width = returned.shape
    return pl.pallas_call(
        output_kernel,
        grid=(groups,),
        in_specs=[
            pl.BlockSpec((rows, HEAD), lambda g: (0, 0)),
            pl.BlockSpec((buffer_rows, width), lambda g: (0, 0)),
            pl.BlockSpec((width, width), lambda g: (g, 0)),
        ],
        out_specs=pl.BlockSpec((1, rows, width), lambda g: (g, 0, 0)),
        out_shape=jax.ShapeDtypeStruct((groups, rows, width), jnp.bfloat16),
        scratch_shapes=[pltpu.VMEM((rows, width), jnp.bfloat16)],
        compiler_params=params(),
        cost_estimate=pl.CostEstimate(
            flops=2 * groups * rows * width * width + 2 * buffer_rows * rows * width,
            bytes_accessed=2 * groups * width * (rows + width),
            transcendentals=0,
        ),
    )(dest_col, returned, weight_t)


def gather_groups(block):
    tp_count = lax.axis_size("tp")
    half = tp_count // 2
    near = [block]
    for shift in range(1, half):
        near.append(lax.ppermute(block, "tp", [(t, (t + 2 * shift) % tp_count) for t in range(tp_count)]))
    near = jnp.stack(near)
    far = lax.ppermute(near, "tp", [(t, t ^ 1) for t in range(tp_count)])
    me = lax.axis_index("tp")
    own = (me + tp_count - 2 * jnp.arange(half, dtype=jnp.int32)) % tp_count
    return jnp.concatenate([near, far], axis=0), jnp.concatenate([own, own ^ 1])


def forward_kernel(scale, chunk, q_ref, k_ref, v_ref, code_ref, mask_ref, att_ref, weight_ref, bias):
    rows = q_ref.shape[0]

    @pl.when(pl.program_id(0) == 0)
    def _():
        lane = lax.broadcasted_iota(jnp.int32, (rows, HEAD), 1).astype(jnp.float32) + 1.0
        onehot = as_bf16(code_ref[...].astype(jnp.float32) == lane)
        linked = dot32(onehot, mask_ref[...]).astype(jnp.bfloat16)
        for start in range(0, rows, chunk):
            linked_part = linked[start : start + chunk]
            allowed = dot32_nt(onehot, linked_part) > 0.5
            bias[:, start : start + chunk] = jnp.where(allowed, 0.0, NEG_FILL)

    value_t = jnp.transpose(v_ref[...])
    for start in range(0, rows, chunk):
        part = slice(start, start + chunk)
        scores = dot32_nt(k_ref[...], q_ref[part, :]) * scale + bias[:, part]
        top = jnp.max(scores, axis=0, keepdims=True)
        terms = jnp.exp(scores - top)
        weights = (terms * (1.0 / jnp.sum(terms, axis=0, keepdims=True))).astype(jnp.bfloat16)
        weight_ref[0, :, part] = weights
        att_ref[part, :] = jnp.transpose(dot32(value_t, weights)).astype(jnp.bfloat16)


def backward_kernel(scale, chunk, q_ref, k_ref, v_ref, att_ref, g_ref, weight_ref, out_ref):
    rows = q_ref.shape[0]
    grad = g_ref[...]
    delta = jnp.sum(
        jnp.transpose(grad.astype(jnp.float32) * att_ref[...].astype(jnp.float32)), axis=0, keepdims=True
    )
    key_t = jnp.transpose(k_ref[...])
    grad_key = jnp.zeros((rows, HEAD), jnp.float32)
    grad_value = jnp.zeros((rows, HEAD), jnp.float32)
    for start in range(0, rows, chunk):
        part = slice(start, start + chunk)
        weights = weight_ref[0, :, part]
        grad_part = g_ref[part, :]
        grad_probs = dot32_nt(v_ref[...], grad_part)
        grad_scores = (weights.astype(jnp.float32) * (grad_probs - delta[:, part])).astype(jnp.bfloat16)
        out_ref[part, 0:HEAD] = jnp.transpose(dot32(key_t, grad_scores) * scale).astype(jnp.bfloat16)
        grad_key = grad_key + dot32(grad_scores, q_ref[part, :])
        grad_value = grad_value + dot32(weights, grad_part)
    out_ref[:, HEAD : 2 * HEAD] = (grad_key * scale).astype(jnp.bfloat16)
    out_ref[:, 2 * HEAD :] = grad_value.astype(jnp.bfloat16)


def attention_forward(owned, pair_mask, heads, scale, chunk):
    rows = owned.shape[0]
    block = (rows, HEAD)
    return pl.pallas_call(
        lambda *refs: forward_kernel(scale, chunk, *refs),
        grid=(heads,),
        in_specs=[
            pl.BlockSpec(block, lambda h: (0, h)),
            pl.BlockSpec(block, lambda h: (0, heads + h)),
            pl.BlockSpec(block, lambda h: (0, 2 * heads + h)),
            pl.BlockSpec(block, lambda h: (0, 3 * heads)),
            pl.BlockSpec(pair_mask.shape, lambda h: (0, 0)),
        ],
        out_specs=(
            pl.BlockSpec(block, lambda h: (0, h)),
            pl.BlockSpec((1, rows, rows), lambda h: (h, 0, 0)),
        ),
        out_shape=(
            jax.ShapeDtypeStruct((rows, heads * HEAD), jnp.bfloat16),
            jax.ShapeDtypeStruct((heads, rows, rows), jnp.bfloat16),
        ),
        scratch_shapes=[pltpu.VMEM((rows, rows), jnp.float32)],
        compiler_params=params(),
        cost_estimate=pl.CostEstimate(
            flops=heads * 4 * rows * rows * HEAD,
            bytes_accessed=heads * rows * (8 * HEAD + 2 * rows),
            transcendentals=heads * rows * rows,
        ),
    )(owned, owned, owned, owned, pair_mask)


def attention_backward(owned, attended, grad_owned, weights, heads, scale, chunk):
    rows = owned.shape[0]
    block = (rows, HEAD)
    return pl.pallas_call(
        lambda *refs: backward_kernel(scale, chunk, *refs),
        grid=(heads,),
        in_specs=[
            pl.BlockSpec(block, lambda h: (0, h)),
            pl.BlockSpec(block, lambda h: (0, heads + h)),
            pl.BlockSpec(block, lambda h: (0, 2 * heads + h)),
            pl.BlockSpec(block, lambda h: (0, h)),
            pl.BlockSpec(block, lambda h: (0, h)),
            pl.BlockSpec((1, rows, rows), lambda h: (h, 0, 0)),
        ],
        out_specs=pl.BlockSpec((rows, 3 * HEAD), lambda h: (0, h)),
        out_shape=jax.ShapeDtypeStruct((rows, 3 * heads * HEAD), jnp.bfloat16),
        compiler_params=params(),
        cost_estimate=pl.CostEstimate(
            flops=heads * 8 * rows * rows * HEAD,
            bytes_accessed=heads * rows * (16 * HEAD + 2 * rows),
            transcendentals=0,
        ),
    )(owned, owned, owned, attended, grad_owned, weights)


def unpack_kernel(dest_ref, blocks_ref, q_ref, k_ref, v_ref):
    rows = q_ref.shape[0]
    buffer_rows = blocks_ref.shape[0]
    select = as_bf16(dest_ref[:, 0:1] == lax.broadcasted_iota(jnp.int32, (rows, buffer_rows), 1))
    for place, out_ref in enumerate((q_ref, k_ref, v_ref)):
        part = blocks_ref[:, place * HEAD : (place + 1) * HEAD]
        out_ref[...] = dot32(select, part).astype(jnp.bfloat16)


def unpack_grads(dest_col, blocks, heads):
    rows = dest_col.shape[0]
    buffer_rows = blocks.shape[0]
    out = jax.ShapeDtypeStruct((rows, heads * HEAD), jnp.bfloat16)
    return pl.pallas_call(
        unpack_kernel,
        grid=(heads,),
        in_specs=[
            pl.BlockSpec((rows, HEAD), lambda h: (0, 0)),
            pl.BlockSpec((buffer_rows, 3 * HEAD), lambda h: (0, h)),
        ],
        out_specs=[pl.BlockSpec((rows, HEAD), lambda h: (0, h))] * 3,
        out_shape=(out, out, out),
        compiler_params=params(),
        cost_estimate=pl.CostEstimate(
            flops=6 * heads * rows * buffer_rows * HEAD,
            bytes_accessed=6 * heads * HEAD * (rows + buffer_rows),
            transcendentals=0,
        ),
    )(dest_col, blocks)


def exchange(matrix, seq_count):
    rows, cols = matrix.shape
    blocks = matrix.reshape(seq_count, rows // seq_count, cols)
    return lax.all_to_all(blocks, "seq", split_axis=0, concat_axis=0, tiled=True).reshape(rows, cols)


def body(queries, key_rows, values, out_weight, grad_out, labels, owner_map, pair_mask):
    seq_count = lax.axis_size("seq")
    row_count, width = queries.shape
    heads = width // HEAD
    slot_size = 2 * row_count // seq_count
    buffer_rows = seq_count * slot_size
    scale = HEAD ** (-0.5)
    chunk = 256
    weight_t = lax.all_gather(out_weight.T, "seq", axis=0, tiled=True)
    grad_blocks, order = gather_groups(grad_out)
    packed, dest_row, dest_col = pack_inputs(
        seq_count, slot_size, labels, owner_map, queries, key_rows, values
    )
    owned = exchange(packed, seq_count)
    attended, weights = attention_forward(owned, pair_mask.astype(jnp.bfloat16), heads, scale, chunk)
    returned = exchange(attended, seq_count)
    grad_owned = exchange(project_grads(order, grad_blocks, weight_t, dest_row, buffer_rows), seq_count)
    partial_out = project_output(dest_col, returned, weight_t, lax.axis_size("tp"))
    output = lax.psum_scatter(partial_out, "tp", scatter_dimension=0, tiled=False)
    grads = attention_backward(owned, attended, grad_owned, weights, heads, scale, chunk)
    back = exchange(grads, seq_count)
    grad_q, grad_k, grad_v = unpack_grads(dest_col, back, heads)
    return (output, grad_q, grad_k, grad_v)


def solution(mesh):
    in_specs = (
        P("seq", "tp"),
        P("seq", "tp"),
        P("seq", "tp"),
        P("tp", "seq"),
        P("seq", "tp"),
        P("seq"),
        P(),
        P(),
    )
    out_specs = (P("seq", "tp"), P("seq", "tp"), P("seq", "tp"), P("seq", "tp"))
    return jax.shard_map(body, mesh=mesh, in_specs=in_specs, out_specs=out_specs, check_vma=False)
```

```python
import jax
import jax.numpy as jnp
from jax import lax
from jax.experimental import pallas as pl
from jax.experimental.pallas import tpu as pltpu
from jax.sharding import PartitionSpec as P

HEAD = 128
NEG_FILL = -1e30
LOG2_E = 1.4426950408889634
VMEM_BYTES = 48 * 1024 * 1024
VMEM_WHOLE = 60 * 1024 * 1024
NT = (((1,), (1,)), ((), ()))


def dot32(left, right):
    return jnp.dot(left, right, preferred_element_type=jnp.float32)


def dot32_nt(left, right):
    return lax.dot_general(left, right, NT, preferred_element_type=jnp.float32)


def params(limit=VMEM_BYTES):
    return pltpu.CompilerParams(vmem_limit_bytes=limit)


def as_bf16(flags):
    return flags.astype(jnp.float32).astype(jnp.bfloat16)


def column_of(row):
    wide = jnp.broadcast_to(row.astype(jnp.float32), (HEAD, row.shape[1]))
    return jnp.transpose(wide)


def pack_kernel(
    seq_count, slot_size, label_row, owner_row_ref, q_ref, k_ref, v_ref, packed, dest_row, dest_col, held, parts, in_sems, out_sems
):
    sources = (q_ref, k_ref, v_ref)
    rows, cols = q_ref.shape
    clusters = owner_row_ref.shape[1]
    buffer_rows = packed.shape[0]
    loads = [pltpu.make_async_copy(ref, held.at[i], in_sems.at[i]) for i, ref in enumerate(sources)]
    for load in loads:
        load.start()
    labels = label_row[...]
    owner_col = column_of(owner_row_ref[...])[:, 0:1].astype(jnp.int32)
    in_cluster = labels == lax.broadcasted_iota(jnp.int32, (clusters, rows), 0)
    owner_row = jnp.sum(jnp.where(in_cluster, owner_col, 0), axis=0, keepdims=True)
    owned = owner_row == lax.broadcasted_iota(jnp.int32, (seq_count, rows), 0)
    earlier = lax.broadcasted_iota(jnp.int32, (rows, rows), 0) < lax.broadcasted_iota(
        jnp.int32, (rows, rows), 1
    )
    before = dot32(as_bf16(owned), as_bf16(earlier))
    rank_row = jnp.sum(jnp.where(owned, before, 0.0), axis=0, keepdims=True)
    dest = owner_row * slot_size + rank_row.astype(jnp.int32)
    dest_row[...] = dest
    dest_col[...] = column_of(dest).astype(jnp.int32)
    select = as_bf16(lax.broadcasted_iota(jnp.int32, (buffer_rows, rows), 0) == dest)
    width = 3 * cols
    parts[:, width:] = dot32(select, column_of(labels + 1).astype(jnp.bfloat16)).astype(jnp.bfloat16)
    stores = []
    for i, load in enumerate(loads):
        load.wait()
        parts[:, i * cols : (i + 1) * cols] = dot32(select, held[i]).astype(jnp.bfloat16)
        part = slice(i * cols, (i + 1) * cols if i < 2 else width + HEAD)
        stores.append(pltpu.make_async_copy(parts.at[:, part], packed.at[:, part], out_sems.at[i]))
        stores[-1].start()
    for store in stores:
        store.wait()


def pack_inputs(seq_count, slot_size, labels, owner_map, queries, key_rows, values):
    rows, cols = queries.shape
    buffer_rows = seq_count * slot_size
    return pl.pallas_call(
        lambda *refs: pack_kernel(seq_count, slot_size, *refs),
        out_shape=(
            jax.ShapeDtypeStruct((buffer_rows, 3 * cols + HEAD), jnp.bfloat16),
            jax.ShapeDtypeStruct((1, rows), jnp.int32),
            jax.ShapeDtypeStruct((rows, HEAD), jnp.int32),
        ),
        in_specs=[pl.BlockSpec(memory_space=pltpu.VMEM)] * 2 + [pl.BlockSpec(memory_space=pl.ANY)] * 3,
        out_specs=(pl.BlockSpec(memory_space=pl.ANY),) + (pl.BlockSpec(memory_space=pltpu.VMEM),) * 2,
        scratch_shapes=[
            pltpu.VMEM((3, rows, cols), jnp.bfloat16),
            pltpu.VMEM((buffer_rows, 3 * cols + HEAD), jnp.bfloat16),
            pltpu.SemaphoreType.DMA((3,)),
            pltpu.SemaphoreType.DMA((3,)),
        ],
        compiler_params=params(VMEM_WHOLE),
    )(labels[None, :], owner_map[None, :], queries, key_rows, values)


def grad_kernel(order_ref, grad_ref, weight_ref, dest_row, packed, total):
    step = pl.program_id(0)

    @pl.when(step == 0)
    def _():
        total[...] = jnp.zeros_like(total)

    total[...] += dot32(grad_ref[0], weight_ref[...])

    @pl.when(step == pl.num_programs(0) - 1)
    def _():
        select = as_bf16(lax.broadcasted_iota(jnp.int32, (packed.shape[0], total.shape[0]), 0) == dest_row[...])
        packed[...] = dot32(select, total[...].astype(jnp.bfloat16)).astype(jnp.bfloat16)


def project_grads(order, grad_blocks, weight_t, dest_row, buffer_rows):
    groups, rows, width = grad_blocks.shape
    return pl.pallas_call(
        grad_kernel,
        grid_spec=pltpu.PrefetchScalarGridSpec(
            num_scalar_prefetch=1,
            grid=(groups,),
            in_specs=[
                pl.BlockSpec((1, rows, width), lambda g, order: (g, 0, 0)),
                pl.BlockSpec((width, width), lambda g, order: (order[g], 0)),
                pl.BlockSpec((1, rows), lambda g, order: (0, 0)),
            ],
            out_specs=pl.BlockSpec((buffer_rows, width), lambda g, order: (0, 0)),
            scratch_shapes=[pltpu.VMEM((rows, width), jnp.float32)],
        ),
        out_shape=jax.ShapeDtypeStruct((buffer_rows, width), jnp.bfloat16),
        compiler_params=params(VMEM_WHOLE),
        cost_estimate=pl.CostEstimate(
            flops=2 * groups * rows * width * width + 2 * buffer_rows * rows * width,
            bytes_accessed=2 * groups * width * (rows + width),
            transcendentals=0,
        ),
    )(order, grad_blocks, weight_t, dest_row)


def output_kernel(dest_col, returned, weight_ref, out_ref, local):
    @pl.when(pl.program_id(0) == 0)
    def _():
        place = lax.broadcasted_iota(jnp.int32, (local.shape[0], returned.shape[0]), 1)
        local[...] = dot32(as_bf16(dest_col[:, 0:1] == place), returned[...]).astype(jnp.bfloat16)

    out_ref[0] = dot32_nt(local[...], weight_ref[...]).astype(jnp.bfloat16)


def project_output(dest_col, returned, weight_t, groups):
    rows = dest_col.shape[0]
    buffer_rows, width = returned.shape
    return pl.pallas_call(
        output_kernel,
        grid=(groups,),
        in_specs=[
            pl.BlockSpec((rows, HEAD), lambda g: (0, 0)),
            pl.BlockSpec((buffer_rows, width), lambda g: (0, 0)),
            pl.BlockSpec((width, width), lambda g: (g, 0)),
        ],
        out_specs=pl.BlockSpec((1, rows, width), lambda g: (g, 0, 0)),
        out_shape=jax.ShapeDtypeStruct((groups, rows, width), jnp.bfloat16),
        scratch_shapes=[pltpu.VMEM((rows, width), jnp.bfloat16)],
        compiler_params=params(),
        cost_estimate=pl.CostEstimate(
            flops=2 * groups * rows * width * width + 2 * buffer_rows * rows * width,
            bytes_accessed=2 * groups * width * (rows + width),
            transcendentals=0,
        ),
    )(dest_col, returned, weight_t)


def gather_groups(block):
    tp_count = lax.axis_size("tp")
    half = tp_count // 2
    near = [block]
    for shift in range(1, half):
        near.append(lax.ppermute(block, "tp", [(t, (t + 2 * shift) % tp_count) for t in range(tp_count)]))
    near = jnp.stack(near)
    far = lax.ppermute(near, "tp", [(t, t ^ 1) for t in range(tp_count)])
    me = lax.axis_index("tp")
    own = (me + tp_count - 2 * jnp.arange(half, dtype=jnp.int32)) % tp_count
    return jnp.concatenate([near, far], axis=0), jnp.concatenate([own, own ^ 1])


def forward_kernel(scale, q_ref, k_ref, v_ref, code_ref, mask_ref, att_ref, weight_ref, keys, asks):
    rows = q_ref.shape[0]

    @pl.when(pl.program_id(0) == 0)
    def _():
        lane = lax.broadcasted_iota(jnp.int32, (rows, HEAD), 1).astype(jnp.float32) + 1.0
        code = code_ref[...].astype(jnp.float32)
        onehot = as_bf16((code == lane) | (code == 0.0))
        linked = dot32(onehot, mask_ref[...])
        keys[:, HEAD:] = onehot
        asks[:, HEAD:] = jnp.where(linked > 0.5, 0.0, NEG_FILL).astype(jnp.bfloat16)

    keys[:, :HEAD] = k_ref[...]
    asks[:, :HEAD] = q_ref[...]
    scores = dot32_nt(keys[...], asks[...])
    top = jnp.max(scores, axis=0, keepdims=True)
    terms = jnp.exp2((scores - top) * (scale * LOG2_E))
    weights = (terms * (1.0 / jnp.sum(terms, axis=0, keepdims=True))).astype(jnp.bfloat16)
    weight_ref[0] = weights
    att_ref[...] = jnp.transpose(dot32(jnp.transpose(v_ref[...]), weights)).astype(jnp.bfloat16)


def backward_kernel(scale, q_ref, k_ref, v_ref, att_ref, g_ref, weight_ref, out_ref):
    grad = g_ref[...]
    weights = weight_ref[0]
    delta = jnp.sum(
        jnp.transpose(grad.astype(jnp.float32) * att_ref[...].astype(jnp.float32)), axis=0, keepdims=True
    )
    grad_probs = dot32_nt(v_ref[...], grad)
    grad_scores = (weights.astype(jnp.float32) * (grad_probs - delta)).astype(jnp.bfloat16)
    grad_query = dot32(jnp.transpose(k_ref[...]), grad_scores) * scale
    out_ref[:, 0:HEAD] = jnp.transpose(grad_query).astype(jnp.bfloat16)
    out_ref[:, HEAD : 2 * HEAD] = (dot32(grad_scores, q_ref[...]) * scale).astype(jnp.bfloat16)
    out_ref[:, 2 * HEAD :] = dot32(weights, grad).astype(jnp.bfloat16)


def attention_forward(owned, pair_mask, heads, scale):
    rows = owned.shape[0]
    block = (rows, HEAD)
    return pl.pallas_call(
        lambda *refs: forward_kernel(scale, *refs),
        grid=(heads,),
        in_specs=[
            pl.BlockSpec(block, lambda h: (0, h)),
            pl.BlockSpec(block, lambda h: (0, heads + h)),
            pl.BlockSpec(block, lambda h: (0, 2 * heads + h)),
            pl.BlockSpec(block, lambda h: (0, 3 * heads)),
            pl.BlockSpec(pair_mask.shape, lambda h: (0, 0)),
        ],
        out_specs=(
            pl.BlockSpec(block, lambda h: (0, h)),
            pl.BlockSpec((1, rows, rows), lambda h: (h, 0, 0)),
        ),
        out_shape=(
            jax.ShapeDtypeStruct((rows, heads * HEAD), jnp.bfloat16),
            jax.ShapeDtypeStruct((heads, rows, rows), jnp.bfloat16),
        ),
        scratch_shapes=[pltpu.VMEM((rows, 2 * HEAD), jnp.bfloat16)] * 2,
        compiler_params=params(),
        cost_estimate=pl.CostEstimate(
            flops=heads * 4 * rows * rows * HEAD,
            bytes_accessed=heads * rows * (8 * HEAD + 2 * rows),
            transcendentals=heads * rows * rows,
        ),
    )(owned, owned, owned, owned, pair_mask)


def attention_backward(owned, attended, grad_owned, weights, heads, scale):
    rows = owned.shape[0]
    block = (rows, HEAD)
    return pl.pallas_call(
        lambda *refs: backward_kernel(scale, *refs),
        grid=(heads,),
        in_specs=[
            pl.BlockSpec(block, lambda h: (0, h)),
            pl.BlockSpec(block, lambda h: (0, heads + h)),
            pl.BlockSpec(block, lambda h: (0, 2 * heads + h)),
            pl.BlockSpec(block, lambda h: (0, h)),
            pl.BlockSpec(block, lambda h: (0, h)),
            pl.BlockSpec((1, rows, rows), lambda h: (h, 0, 0)),
        ],
        out_specs=pl.BlockSpec((rows, 3 * HEAD), lambda h: (0, h)),
        out_shape=jax.ShapeDtypeStruct((rows, 3 * heads * HEAD), jnp.bfloat16),
        compiler_params=params(),
        cost_estimate=pl.CostEstimate(
            flops=heads * 8 * rows * rows * HEAD,
            bytes_accessed=heads * rows * (16 * HEAD + 2 * rows),
            transcendentals=0,
        ),
    )(owned, owned, owned, attended, grad_owned, weights)


def unpack_kernel(dest_ref, blocks_ref, q_ref, k_ref, v_ref, select):
    @pl.when(pl.program_id(0) == 0)
    def _():
        select[...] = as_bf16(dest_ref[:, 0:1] == lax.broadcasted_iota(jnp.int32, select.shape, 1))

    picked = dot32(select[...], blocks_ref[...]).astype(jnp.bfloat16)
    q_ref[...] = picked[:, 0:HEAD]
    k_ref[...] = picked[:, HEAD : 2 * HEAD]
    v_ref[...] = picked[:, 2 * HEAD :]


def unpack_grads(dest_col, blocks, heads):
    rows = dest_col.shape[0]
    buffer_rows = blocks.shape[0]
    out = jax.ShapeDtypeStruct((rows, heads * HEAD), jnp.bfloat16)
    return pl.pallas_call(
        unpack_kernel,
        grid=(heads,),
        in_specs=[
            pl.BlockSpec((rows, HEAD), lambda h: (0, 0)),
            pl.BlockSpec((buffer_rows, 3 * HEAD), lambda h: (0, h)),
        ],
        out_specs=[pl.BlockSpec((rows, HEAD), lambda h: (0, h))] * 3,
        out_shape=(out, out, out),
        scratch_shapes=[pltpu.VMEM((rows, buffer_rows), jnp.bfloat16)],
        compiler_params=params(),
        cost_estimate=pl.CostEstimate(
            flops=6 * heads * rows * buffer_rows * HEAD,
            bytes_accessed=6 * heads * HEAD * (rows + buffer_rows),
            transcendentals=0,
        ),
    )(dest_col, blocks)


def exchange(matrix, seq_count):
    rows, cols = matrix.shape
    blocks = matrix.reshape(seq_count, rows // seq_count, cols)
    return lax.all_to_all(blocks, "seq", split_axis=0, concat_axis=0, tiled=True).reshape(rows, cols)


def body(queries, key_rows, values, out_weight, grad_out, labels, owner_map, pair_mask):
    seq_count = lax.axis_size("seq")
    row_count, width = queries.shape
    heads = width // HEAD
    slot_size = 2 * row_count // seq_count
    buffer_rows = seq_count * slot_size
    scale = HEAD ** (-0.5)
    weight_t = lax.all_gather(out_weight.T, "seq", axis=0, tiled=True)
    grad_blocks, order = gather_groups(grad_out)
    packed, dest_row, dest_col = pack_inputs(
        seq_count, slot_size, labels, owner_map, queries, key_rows, values
    )
    owned = exchange(packed, seq_count)
    attended, weights = attention_forward(owned, pair_mask.astype(jnp.bfloat16), heads, scale)
    returned = exchange(attended, seq_count)
    grad_owned = exchange(project_grads(order, grad_blocks, weight_t, dest_row, buffer_rows), seq_count)
    partial_out = project_output(dest_col, returned, weight_t, lax.axis_size("tp"))
    output = lax.psum_scatter(partial_out, "tp", scatter_dimension=0, tiled=False)
    grads = attention_backward(owned, attended, grad_owned, weights, heads, scale)
    back = exchange(grads, seq_count)
    grad_q, grad_k, grad_v = unpack_grads(dest_col, back, heads)
    return (output, grad_q, grad_k, grad_v)


def solution(mesh):
    in_specs = (
        P("seq", "tp"),
        P("seq", "tp"),
        P("seq", "tp"),
        P("tp", "seq"),
        P("seq", "tp"),
        P("seq"),
        P(),
        P(),
    )
    out_specs = (P("seq", "tp"), P("seq", "tp"), P("seq", "tp"), P("seq", "tp"))
    return jax.shard_map(body, mesh=mesh, in_specs=in_specs, out_specs=out_specs, check_vma=False)
```

```python
import jax
import jax.numpy as jnp
from jax import lax
from jax.experimental import pallas as pl
from jax.experimental.pallas import tpu as pltpu
from jax.sharding import PartitionSpec as P

HEAD = 128
NEG_FILL = -1e30
LOG2_E = 1.4426950408889634
VMEM_BYTES = 48 * 1024 * 1024
VMEM_WHOLE = 60 * 1024 * 1024
NT = (((1,), (1,)), ((), ()))


def dot32(left, right):
    return jnp.dot(left, right, preferred_element_type=jnp.float32)


def dot32_nt(left, right):
    return lax.dot_general(left, right, NT, preferred_element_type=jnp.float32)


def params(limit=VMEM_BYTES):
    return pltpu.CompilerParams(vmem_limit_bytes=limit)


def as_bf16(flags):
    return flags.astype(jnp.float32).astype(jnp.bfloat16)


def column_of(row):
    wide = jnp.broadcast_to(row.astype(jnp.float32), (HEAD, row.shape[1]))
    return jnp.transpose(wide)


def pack_kernel(
    seq_count, slot_size, label_row, owner_row_ref, q_ref, k_ref, v_ref, packed, dest_row, dest_col, held, parts, in_sems, out_sems
):
    sources = (q_ref, k_ref, v_ref)
    rows, cols = q_ref.shape
    clusters = owner_row_ref.shape[1]
    buffer_rows = packed.shape[0]
    loads = [pltpu.make_async_copy(ref, held.at[i], in_sems.at[i]) for i, ref in enumerate(sources)]
    for load in loads:
        load.start()
    labels = label_row[...].reshape(1, rows)
    owner_col = column_of(owner_row_ref[...])[:, 0:1].astype(jnp.int32)
    in_cluster = labels == lax.broadcasted_iota(jnp.int32, (clusters, rows), 0)
    owner_row = jnp.sum(jnp.where(in_cluster, owner_col, 0), axis=0, keepdims=True)
    owned = owner_row == lax.broadcasted_iota(jnp.int32, (seq_count, rows), 0)
    earlier = lax.broadcasted_iota(jnp.int32, (rows, rows), 0) < lax.broadcasted_iota(
        jnp.int32, (rows, rows), 1
    )
    before = dot32(as_bf16(owned), as_bf16(earlier))
    rank_row = jnp.sum(jnp.where(owned, before, 0.0), axis=0, keepdims=True)
    dest = owner_row * slot_size + rank_row.astype(jnp.int32)
    dest_row[...] = dest
    select = as_bf16(lax.broadcasted_iota(jnp.int32, (buffer_rows, rows), 0) == dest)
    width = 3 * cols
    stores = []

    def store(start, stop):
        part = slice(start, stop)
        stores.append(pltpu.make_async_copy(parts.at[:, part], packed.at[:, part], out_sems.at[len(stores)]))
        stores[-1].start()

    for i, load in enumerate(loads):
        load.wait()
        parts[:, i * cols : (i + 1) * cols] = dot32(select, held[i]).astype(jnp.bfloat16)
        store(i * cols, (i + 1) * cols)
    parts[:, width:] = dot32(select, column_of(labels + 1).astype(jnp.bfloat16)).astype(jnp.bfloat16)
    store(width, width + HEAD)
    dest_col[...] = column_of(dest).astype(jnp.int32)
    for copy in stores:
        copy.wait()


def pack_inputs(seq_count, slot_size, labels, owner_map, queries, key_rows, values):
    rows, cols = queries.shape
    buffer_rows = seq_count * slot_size
    return pl.pallas_call(
        lambda *refs: pack_kernel(seq_count, slot_size, *refs),
        out_shape=(
            jax.ShapeDtypeStruct((buffer_rows, 3 * cols + HEAD), jnp.bfloat16),
            jax.ShapeDtypeStruct((1, rows), jnp.int32),
            jax.ShapeDtypeStruct((rows, HEAD), jnp.int32),
        ),
        in_specs=[pl.BlockSpec(memory_space=pltpu.VMEM)] * 2 + [pl.BlockSpec(memory_space=pl.ANY)] * 3,
        out_specs=(pl.BlockSpec(memory_space=pl.ANY),) + (pl.BlockSpec(memory_space=pltpu.VMEM),) * 2,
        scratch_shapes=[
            pltpu.VMEM((3, rows, cols), jnp.bfloat16),
            pltpu.VMEM((buffer_rows, 3 * cols + HEAD), jnp.bfloat16),
            pltpu.SemaphoreType.DMA((3,)),
            pltpu.SemaphoreType.DMA((4,)),
        ],
        compiler_params=params(VMEM_WHOLE),
    )(labels, owner_map[None, :], queries, key_rows, values)


def grad_kernel(order_ref, grad_ref, weight_ref, dest_row, packed, total):
    step = pl.program_id(0)

    @pl.when(step == 0)
    def _():
        total[...] = jnp.zeros_like(total)

    total[...] += dot32(grad_ref[0], weight_ref[...])

    @pl.when(step == pl.num_programs(0) - 1)
    def _():
        select = as_bf16(lax.broadcasted_iota(jnp.int32, (packed.shape[0], total.shape[0]), 0) == dest_row[...])
        packed[...] = dot32(select, total[...].astype(jnp.bfloat16)).astype(jnp.bfloat16)


def project_grads(order, grad_blocks, weight_t, dest_row, buffer_rows):
    groups, rows, width = grad_blocks.shape
    return pl.pallas_call(
        grad_kernel,
        grid_spec=pltpu.PrefetchScalarGridSpec(
            num_scalar_prefetch=1,
            grid=(groups,),
            in_specs=[
                pl.BlockSpec((1, rows, width), lambda g, order: (g, 0, 0)),
                pl.BlockSpec((width, width), lambda g, order: (order[g], 0)),
                pl.BlockSpec((1, rows), lambda g, order: (0, 0)),
            ],
            out_specs=pl.BlockSpec((buffer_rows, width), lambda g, order: (0, 0)),
            scratch_shapes=[pltpu.VMEM((rows, width), jnp.float32)],
        ),
        out_shape=jax.ShapeDtypeStruct((buffer_rows, width), jnp.bfloat16),
        compiler_params=params(VMEM_WHOLE),
        cost_estimate=pl.CostEstimate(
            flops=2 * groups * rows * width * width + 2 * buffer_rows * rows * width,
            bytes_accessed=2 * groups * width * (rows + width),
            transcendentals=0,
        ),
    )(order, grad_blocks, weight_t, dest_row)


def output_kernel(dest_col, returned, weight_ref, out_ref, local):
    @pl.when(pl.program_id(0) == 0)
    def _():
        place = lax.broadcasted_iota(jnp.int32, (local.shape[0], returned.shape[0]), 1)
        local[...] = dot32(as_bf16(dest_col[:, 0:1] == place), returned[...]).astype(jnp.bfloat16)

    out_ref[0] = dot32_nt(local[...], weight_ref[...]).astype(jnp.bfloat16)


def project_output(dest_col, returned, weight_t, groups):
    rows = dest_col.shape[0]
    buffer_rows, width = returned.shape
    return pl.pallas_call(
        output_kernel,
        grid=(groups,),
        in_specs=[
            pl.BlockSpec((rows, HEAD), lambda g: (0, 0)),
            pl.BlockSpec((buffer_rows, width), lambda g: (0, 0)),
            pl.BlockSpec((width, width), lambda g: (g, 0)),
        ],
        out_specs=pl.BlockSpec((1, rows, width), lambda g: (g, 0, 0)),
        out_shape=jax.ShapeDtypeStruct((groups, rows, width), jnp.bfloat16),
        scratch_shapes=[pltpu.VMEM((rows, width), jnp.bfloat16)],
        compiler_params=params(),
        cost_estimate=pl.CostEstimate(
            flops=2 * groups * rows * width * width + 2 * buffer_rows * rows * width,
            bytes_accessed=2 * groups * width * (rows + width),
            transcendentals=0,
        ),
    )(dest_col, returned, weight_t)


def gather_groups(block):
    tp_count = lax.axis_size("tp")
    half = tp_count // 2
    near = [block]
    for shift in range(1, half):
        near.append(lax.ppermute(block, "tp", [(t, (t + 2 * shift) % tp_count) for t in range(tp_count)]))
    near = jnp.stack(near)
    far = lax.ppermute(near, "tp", [(t, t ^ 1) for t in range(tp_count)])
    me = lax.axis_index("tp")
    own = (me + tp_count - 2 * jnp.arange(half, dtype=jnp.int32)) % tp_count
    return jnp.concatenate([near, far], axis=0), jnp.concatenate([own, own ^ 1])


def forward_kernel(scale, q_ref, k_ref, v_ref, code_ref, mask_ref, att_ref, weight_ref, keys, asks):
    rows = q_ref.shape[0]

    @pl.when(pl.program_id(0) == 0)
    def _():
        lane = lax.broadcasted_iota(jnp.int32, (rows, HEAD), 1).astype(jnp.float32) + 1.0
        code = code_ref[...].astype(jnp.float32)
        onehot = as_bf16((code == lane) | (code == 0.0))
        linked = dot32(onehot, mask_ref[...])
        keys[:, HEAD:] = onehot
        asks[:, HEAD:] = jnp.where(linked > 0.5, 0.0, NEG_FILL).astype(jnp.bfloat16)

    keys[:, :HEAD] = k_ref[...]
    asks[:, :HEAD] = q_ref[...]
    scores = dot32_nt(keys[...], asks[...])
    top = jnp.max(scores, axis=0, keepdims=True)
    terms = jnp.exp2((scores - top) * (scale * LOG2_E))
    weights = (terms * (1.0 / jnp.sum(terms, axis=0, keepdims=True))).astype(jnp.bfloat16)
    weight_ref[0] = weights
    att_ref[...] = jnp.transpose(dot32(jnp.transpose(v_ref[...]), weights)).astype(jnp.bfloat16)


def backward_kernel(scale, q_ref, k_ref, v_ref, att_ref, g_ref, weight_ref, out_ref):
    grad = g_ref[...]
    weights = weight_ref[0]
    delta = jnp.sum(
        jnp.transpose(grad.astype(jnp.float32) * att_ref[...].astype(jnp.float32)), axis=0, keepdims=True
    )
    grad_probs = dot32_nt(v_ref[...], grad)
    grad_scores = (weights.astype(jnp.float32) * (grad_probs - delta)).astype(jnp.bfloat16)
    grad_query = dot32(jnp.transpose(k_ref[...]), grad_scores) * scale
    out_ref[:, 0:HEAD] = jnp.transpose(grad_query).astype(jnp.bfloat16)
    out_ref[:, HEAD : 2 * HEAD] = (dot32(grad_scores, q_ref[...]) * scale).astype(jnp.bfloat16)
    out_ref[:, 2 * HEAD :] = dot32(weights, grad).astype(jnp.bfloat16)


def attention_forward(owned, pair_mask, heads, scale):
    rows = owned.shape[0]
    block = (rows, HEAD)
    return pl.pallas_call(
        lambda *refs: forward_kernel(scale, *refs),
        grid=(heads,),
        in_specs=[
            pl.BlockSpec(block, lambda h: (0, h)),
            pl.BlockSpec(block, lambda h: (0, heads + h)),
            pl.BlockSpec(block, lambda h: (0, 2 * heads + h)),
            pl.BlockSpec(block, lambda h: (0, 3 * heads)),
            pl.BlockSpec(pair_mask.shape, lambda h: (0, 0)),
        ],
        out_specs=(
            pl.BlockSpec(block, lambda h: (0, h)),
            pl.BlockSpec((1, rows, rows), lambda h: (h, 0, 0)),
        ),
        out_shape=(
            jax.ShapeDtypeStruct((rows, heads * HEAD), jnp.bfloat16),
            jax.ShapeDtypeStruct((heads, rows, rows), jnp.bfloat16),
        ),
        scratch_shapes=[pltpu.VMEM((rows, 2 * HEAD), jnp.bfloat16)] * 2,
        compiler_params=params(),
        cost_estimate=pl.CostEstimate(
            flops=heads * 4 * rows * rows * HEAD,
            bytes_accessed=heads * rows * (8 * HEAD + 2 * rows),
            transcendentals=heads * rows * rows,
        ),
    )(owned, owned, owned, owned, pair_mask)


def attention_backward(owned, attended, grad_owned, weights, heads, scale):
    rows = owned.shape[0]
    block = (rows, HEAD)
    return pl.pallas_call(
        lambda *refs: backward_kernel(scale, *refs),
        grid=(heads,),
        in_specs=[
            pl.BlockSpec(block, lambda h: (0, h)),
            pl.BlockSpec(block, lambda h: (0, heads + h)),
            pl.BlockSpec(block, lambda h: (0, 2 * heads + h)),
            pl.BlockSpec(block, lambda h: (0, h)),
            pl.BlockSpec(block, lambda h: (0, h)),
            pl.BlockSpec((1, rows, rows), lambda h: (h, 0, 0)),
        ],
        out_specs=pl.BlockSpec((rows, 3 * HEAD), lambda h: (0, h)),
        out_shape=jax.ShapeDtypeStruct((rows, 3 * heads * HEAD), jnp.bfloat16),
        compiler_params=params(),
        cost_estimate=pl.CostEstimate(
            flops=heads * 8 * rows * rows * HEAD,
            bytes_accessed=heads * rows * (16 * HEAD + 2 * rows),
            transcendentals=0,
        ),
    )(owned, owned, owned, attended, grad_owned, weights)


def unpack_kernel(dest_ref, blocks_ref, q_ref, k_ref, v_ref, select):
    @pl.when(pl.program_id(0) == 0)
    def _():
        select[...] = as_bf16(dest_ref[:, 0:1] == lax.broadcasted_iota(jnp.int32, select.shape, 1))

    picked = dot32(select[...], blocks_ref[...]).astype(jnp.bfloat16)
    q_ref[...] = picked[:, 0:HEAD]
    k_ref[...] = picked[:, HEAD : 2 * HEAD]
    v_ref[...] = picked[:, 2 * HEAD :]


def unpack_grads(dest_col, blocks, heads):
    rows = dest_col.shape[0]
    buffer_rows = blocks.shape[0]
    out = jax.ShapeDtypeStruct((rows, heads * HEAD), jnp.bfloat16)
    return pl.pallas_call(
        unpack_kernel,
        grid=(heads,),
        in_specs=[
            pl.BlockSpec((rows, HEAD), lambda h: (0, 0)),
            pl.BlockSpec((buffer_rows, 3 * HEAD), lambda h: (0, h)),
        ],
        out_specs=[pl.BlockSpec((rows, HEAD), lambda h: (0, h))] * 3,
        out_shape=(out, out, out),
        scratch_shapes=[pltpu.VMEM((rows, buffer_rows), jnp.bfloat16)],
        compiler_params=params(),
        cost_estimate=pl.CostEstimate(
            flops=6 * heads * rows * buffer_rows * HEAD,
            bytes_accessed=6 * heads * HEAD * (rows + buffer_rows),
            transcendentals=0,
        ),
    )(dest_col, blocks)


def exchange(matrix, seq_count):
    rows, cols = matrix.shape
    blocks = matrix.reshape(seq_count, rows // seq_count, cols)
    return lax.all_to_all(blocks, "seq", split_axis=0, concat_axis=0, tiled=True).reshape(rows, cols)


def body(queries, key_rows, values, out_weight, grad_out, labels, owner_map, pair_mask):
    seq_count = lax.axis_size("seq")
    row_count, width = queries.shape
    heads = width // HEAD
    slot_size = 2 * row_count // seq_count
    buffer_rows = seq_count * slot_size
    scale = HEAD ** (-0.5)
    weight_t = lax.all_gather(out_weight.T, "seq", axis=0, tiled=True)
    grad_blocks, order = gather_groups(grad_out)
    packed, dest_row, dest_col = pack_inputs(
        seq_count, slot_size, labels, owner_map, queries, key_rows, values
    )
    owned = exchange(packed, seq_count)
    attended, weights = attention_forward(owned, pair_mask.astype(jnp.bfloat16), heads, scale)
    returned = exchange(attended, seq_count)
    grad_owned = exchange(project_grads(order, grad_blocks, weight_t, dest_row, buffer_rows), seq_count)
    partial_out = project_output(dest_col, returned, weight_t, lax.axis_size("tp"))
    output = lax.psum_scatter(partial_out, "tp", scatter_dimension=0, tiled=False)
    grads = attention_backward(owned, attended, grad_owned, weights, heads, scale)
    back = exchange(grads, seq_count)
    grad_q, grad_k, grad_v = unpack_grads(dest_col, back, heads)
    return (output, grad_q, grad_k, grad_v)


def solution(mesh):
    in_specs = (
        P("seq", "tp"),
        P("seq", "tp"),
        P("seq", "tp"),
        P("tp", "seq"),
        P("seq", "tp"),
        P("seq"),
        P(),
        P(),
    )
    out_specs = (P("seq", "tp"), P("seq", "tp"), P("seq", "tp"), P("seq", "tp"))
    return jax.shard_map(body, mesh=mesh, in_specs=in_specs, out_specs=out_specs, check_vma=False)
```

```python
import jax
import jax.numpy as jnp
from jax import lax
from jax.experimental import pallas as pl
from jax.experimental.pallas import tpu as pltpu
from jax.sharding import PartitionSpec as P

HEAD = 128
NEG_FILL = -1e30
LOG2_E = 1.4426950408889634
Y_COUNT = 4
Z_COUNT = 8
VMEM_BYTES = 48 * 1024 * 1024
VMEM_WHOLE = 60 * 1024 * 1024
NT = (((1,), (1,)), ((), ()))


def dot32(left, right):
    return jnp.dot(left, right, preferred_element_type=jnp.float32)


def dot32_nt(left, right):
    return lax.dot_general(left, right, NT, preferred_element_type=jnp.float32)


def params(limit=VMEM_BYTES):
    return pltpu.CompilerParams(vmem_limit_bytes=limit)


def as_bf16(flags):
    return flags.astype(jnp.float32).astype(jnp.bfloat16)


def column_of(row):
    wide = jnp.broadcast_to(row.astype(jnp.float32), (HEAD, row.shape[1]))
    return jnp.transpose(wide)


def pack_kernel(
    seq_count, slot_size, label_row, owner_row_ref, q_ref, k_ref, v_ref, packed, dest_row, dest_col, code_row, held, parts, in_sems, out_sems
):
    sources = (q_ref, k_ref, v_ref)
    rows, cols = q_ref.shape
    clusters = owner_row_ref.shape[1]
    buffer_rows = packed.shape[0]
    loads = [pltpu.make_async_copy(ref, held.at[i], in_sems.at[i]) for i, ref in enumerate(sources)]
    for load in loads:
        load.start()
    labels = label_row[...].reshape(1, rows)
    owner_col = column_of(owner_row_ref[...])[:, 0:1].astype(jnp.int32)
    in_cluster = labels == lax.broadcasted_iota(jnp.int32, (clusters, rows), 0)
    owner_row = jnp.sum(jnp.where(in_cluster, owner_col, 0), axis=0, keepdims=True)
    owned = owner_row == lax.broadcasted_iota(jnp.int32, (seq_count, rows), 0)
    earlier = lax.broadcasted_iota(jnp.int32, (rows, rows), 0) < lax.broadcasted_iota(
        jnp.int32, (rows, rows), 1
    )
    before = dot32(as_bf16(owned), as_bf16(earlier))
    rank_row = jnp.sum(jnp.where(owned, before, 0.0), axis=0, keepdims=True)
    dest = owner_row * slot_size + rank_row.astype(jnp.int32)
    dest_row[...] = dest
    select = as_bf16(lax.broadcasted_iota(jnp.int32, (buffer_rows, rows), 0) == dest)
    stores = []

    def store(start, stop):
        part = slice(start, stop)
        stores.append(pltpu.make_async_copy(parts.at[:, part], packed.at[:, part], out_sems.at[len(stores)]))
        stores[-1].start()

    for i, load in enumerate(loads):
        load.wait()
        parts[:, i * cols : (i + 1) * cols] = dot32(select, held[i]).astype(jnp.bfloat16)
        store(i * cols, (i + 1) * cols)
    codes = jnp.broadcast_to((labels + 1).astype(jnp.float32), (16, rows)).astype(jnp.bfloat16)
    code_row[...] = dot32_nt(codes, select)[0:1].astype(jnp.int32)
    dest_col[...] = column_of(dest).astype(jnp.int32)
    for copy in stores:
        copy.wait()


def pack_inputs(seq_count, slot_size, labels, owner_map, queries, key_rows, values):
    rows, cols = queries.shape
    buffer_rows = seq_count * slot_size
    return pl.pallas_call(
        lambda *refs: pack_kernel(seq_count, slot_size, *refs),
        out_shape=(
            jax.ShapeDtypeStruct((buffer_rows, 3 * cols), jnp.bfloat16),
            jax.ShapeDtypeStruct((1, rows), jnp.int32),
            jax.ShapeDtypeStruct((rows, HEAD), jnp.int32),
            jax.ShapeDtypeStruct((1, buffer_rows), jnp.int32),
        ),
        in_specs=[pl.BlockSpec(memory_space=pltpu.VMEM)] * 2 + [pl.BlockSpec(memory_space=pl.ANY)] * 3,
        out_specs=(pl.BlockSpec(memory_space=pl.ANY),) + (pl.BlockSpec(memory_space=pltpu.VMEM),) * 3,
        scratch_shapes=[
            pltpu.VMEM((3, rows, cols), jnp.bfloat16),
            pltpu.VMEM((buffer_rows, 3 * cols), jnp.bfloat16),
            pltpu.SemaphoreType.DMA((3,)),
            pltpu.SemaphoreType.DMA((3,)),
        ],
        compiler_params=params(VMEM_WHOLE),
    )(labels, owner_map[None, :], queries, key_rows, values)


def grad_kernel(order_ref, near_ref, far_ref, weight_ref, dest_row, packed, total):
    step = pl.program_id(0)
    half = pl.num_programs(0) // 2

    @pl.when(step == 0)
    def _():
        total[...] = jnp.zeros_like(total)

    @pl.when(step < half)
    def _():
        total[...] += dot32(near_ref[0], weight_ref[...])

    @pl.when(step >= half)
    def _():
        total[...] += dot32(far_ref[0], weight_ref[...])

    @pl.when(step == pl.num_programs(0) - 1)
    def _():
        select = as_bf16(lax.broadcasted_iota(jnp.int32, (packed.shape[0], total.shape[0]), 0) == dest_row[...])
        packed[...] = dot32(select, total[...].astype(jnp.bfloat16)).astype(jnp.bfloat16)


def project_grads(order, near, far, weight_t, dest_row, buffer_rows):
    half, rows, width = near.shape
    groups = 2 * half
    return pl.pallas_call(
        grad_kernel,
        grid_spec=pltpu.PrefetchScalarGridSpec(
            num_scalar_prefetch=1,
            grid=(groups,),
            in_specs=[
                pl.BlockSpec((1, rows, width), lambda g, order: (jnp.minimum(g, half - 1), 0, 0)),
                pl.BlockSpec((1, rows, width), lambda g, order: (jnp.maximum(g - half, 0), 0, 0)),
                pl.BlockSpec((width, width), lambda g, order: (order[g], 0)),
                pl.BlockSpec((1, rows), lambda g, order: (0, 0)),
            ],
            out_specs=pl.BlockSpec((buffer_rows, width), lambda g, order: (0, 0)),
            scratch_shapes=[pltpu.VMEM((rows, width), jnp.float32)],
        ),
        out_shape=jax.ShapeDtypeStruct((buffer_rows, width), jnp.bfloat16),
        compiler_params=params(VMEM_WHOLE),
        cost_estimate=pl.CostEstimate(
            flops=2 * groups * rows * width * width + 2 * buffer_rows * rows * width,
            bytes_accessed=2 * groups * width * (rows + width),
            transcendentals=0,
        ),
    )(order, near, far, weight_t, dest_row)


def output_kernel(dest_col, returned, weight_ref, out_ref, local):
    @pl.when(pl.program_id(0) == 0)
    def _():
        place = lax.broadcasted_iota(jnp.int32, (local.shape[0], returned.shape[0]), 1)
        local[...] = dot32(as_bf16(dest_col[:, 0:1] == place), returned[...]).astype(jnp.bfloat16)

    out_ref[0] = dot32_nt(local[...], weight_ref[...]).astype(jnp.bfloat16)


def project_output(dest_col, returned, weight_t, groups):
    rows = dest_col.shape[0]
    buffer_rows, width = returned.shape
    return pl.pallas_call(
        output_kernel,
        grid=(groups,),
        in_specs=[
            pl.BlockSpec((rows, HEAD), lambda g: (0, 0)),
            pl.BlockSpec((buffer_rows, width), lambda g: (0, 0)),
            pl.BlockSpec((width, width), lambda g: (g, 0)),
        ],
        out_specs=pl.BlockSpec((1, rows, width), lambda g: (g, 0, 0)),
        out_shape=jax.ShapeDtypeStruct((groups, rows, width), jnp.bfloat16),
        scratch_shapes=[pltpu.VMEM((rows, width), jnp.bfloat16)],
        compiler_params=params(),
        cost_estimate=pl.CostEstimate(
            flops=2 * groups * rows * width * width + 2 * buffer_rows * rows * width,
            bytes_accessed=2 * groups * width * (rows + width),
            transcendentals=0,
        ),
    )(dest_col, returned, weight_t)


def gather_groups(block):
    tp_count = lax.axis_size("tp")
    half = tp_count // 2
    near = [block]
    for shift in range(1, half):
        near.append(lax.ppermute(block, "tp", [(t, (t + 2 * shift) % tp_count) for t in range(tp_count)]))
    near = jnp.stack(near)
    far = lax.ppermute(near, "tp", [(t, t ^ 1) for t in range(tp_count)])
    me = lax.axis_index("tp")
    own = (me + tp_count - 2 * jnp.arange(half, dtype=jnp.int32)) % tp_count
    return near, far, jnp.concatenate([own, own ^ 1])


def gather_codes(code_row, slot_size):
    def move(block, along_y, along_z):
        steps = [
            (y * Z_COUNT + z, (y + along_y) % Y_COUNT * Z_COUNT + (z + along_z) % Z_COUNT)
            for y in range(Y_COUNT)
            for z in range(Z_COUNT)
        ]
        return lax.ppermute(block, "seq", steps)

    rows = jnp.concatenate([code_row] + [move(code_row, turn, 0) for turn in range(1, Y_COUNT)])
    table = jnp.concatenate([rows] + [move(rows, 0, turn) for turn in range(1, Z_COUNT)])
    me = lax.axis_index("seq")
    mine = lax.dynamic_slice_in_dim(table, me * slot_size, slot_size, 1)
    source = jnp.arange(Y_COUNT * Z_COUNT, dtype=jnp.int32)
    turn_y = (me // Z_COUNT - source // Z_COUNT + Y_COUNT) % Y_COUNT
    turn_z = (me - source + Y_COUNT * Z_COUNT) % Z_COUNT
    codes = mine[turn_z * Y_COUNT + turn_y].reshape(-1, 1)
    return jnp.broadcast_to(codes, (codes.shape[0], HEAD)).astype(jnp.bfloat16)


def forward_kernel(scale, q_ref, k_ref, v_ref, code_ref, mask_ref, att_ref, weight_ref, keys, asks):
    rows = q_ref.shape[0]

    @pl.when(pl.program_id(0) == 0)
    def _():
        lane = lax.broadcasted_iota(jnp.int32, (rows, HEAD), 1).astype(jnp.float32) + 1.0
        code = code_ref[...].astype(jnp.float32)
        onehot = as_bf16((code == lane) | (code == 0.0))
        linked = dot32(onehot, mask_ref[...])
        keys[:, HEAD:] = onehot
        asks[:, HEAD:] = jnp.where(linked > 0.5, 0.0, NEG_FILL).astype(jnp.bfloat16)

    keys[:, :HEAD] = k_ref[...]
    asks[:, :HEAD] = q_ref[...]
    scores = dot32_nt(keys[...], asks[...])
    top = jnp.max(scores, axis=0, keepdims=True)
    terms = jnp.exp2((scores - top) * (scale * LOG2_E))
    weights = (terms * (1.0 / jnp.sum(terms, axis=0, keepdims=True))).astype(jnp.bfloat16)
    weight_ref[0] = weights
    att_ref[...] = jnp.transpose(dot32(jnp.transpose(v_ref[...]), weights)).astype(jnp.bfloat16)


def backward_kernel(scale, q_ref, k_ref, v_ref, att_ref, g_ref, weight_ref, out_ref):
    grad = g_ref[...]
    weights = weight_ref[0]
    delta = jnp.sum(
        jnp.transpose(grad.astype(jnp.float32) * att_ref[...].astype(jnp.float32)), axis=0, keepdims=True
    )
    grad_probs = dot32_nt(v_ref[...], grad)
    grad_scores = (weights.astype(jnp.float32) * (grad_probs - delta)).astype(jnp.bfloat16)
    grad_query = dot32(jnp.transpose(k_ref[...]), grad_scores) * scale
    out_ref[:, 0:HEAD] = jnp.transpose(grad_query).astype(jnp.bfloat16)
    out_ref[:, HEAD : 2 * HEAD] = (dot32(grad_scores, q_ref[...]) * scale).astype(jnp.bfloat16)
    out_ref[:, 2 * HEAD :] = dot32(weights, grad).astype(jnp.bfloat16)


def attention_forward(owned, codes, pair_mask, heads, scale):
    rows = owned.shape[0]
    block = (rows, HEAD)
    return pl.pallas_call(
        lambda *refs: forward_kernel(scale, *refs),
        grid=(heads,),
        in_specs=[
            pl.BlockSpec(block, lambda h: (0, h)),
            pl.BlockSpec(block, lambda h: (0, heads + h)),
            pl.BlockSpec(block, lambda h: (0, 2 * heads + h)),
            pl.BlockSpec(block, lambda h: (0, 0)),
            pl.BlockSpec(pair_mask.shape, lambda h: (0, 0)),
        ],
        out_specs=(
            pl.BlockSpec(block, lambda h: (0, h)),
            pl.BlockSpec((1, rows, rows), lambda h: (h, 0, 0)),
        ),
        out_shape=(
            jax.ShapeDtypeStruct((rows, heads * HEAD), jnp.bfloat16),
            jax.ShapeDtypeStruct((heads, rows, rows), jnp.bfloat16),
        ),
        scratch_shapes=[pltpu.VMEM((rows, 2 * HEAD), jnp.bfloat16)] * 2,
        compiler_params=params(),
        cost_estimate=pl.CostEstimate(
            flops=heads * 4 * rows * rows * HEAD,
            bytes_accessed=heads * rows * (8 * HEAD + 2 * rows),
            transcendentals=heads * rows * rows,
        ),
    )(owned, owned, owned, codes, pair_mask)


def attention_backward(owned, attended, grad_owned, weights, heads, scale):
    rows = owned.shape[0]
    block = (rows, HEAD)
    return pl.pallas_call(
        lambda *refs: backward_kernel(scale, *refs),
        grid=(heads,),
        in_specs=[
            pl.BlockSpec(block, lambda h: (0, h)),
            pl.BlockSpec(block, lambda h: (0, heads + h)),
            pl.BlockSpec(block, lambda h: (0, 2 * heads + h)),
            pl.BlockSpec(block, lambda h: (0, h)),
            pl.BlockSpec(block, lambda h: (0, h)),
            pl.BlockSpec((1, rows, rows), lambda h: (h, 0, 0)),
        ],
        out_specs=pl.BlockSpec((rows, 3 * HEAD), lambda h: (0, h)),
        out_shape=jax.ShapeDtypeStruct((rows, 3 * heads * HEAD), jnp.bfloat16),
        compiler_params=params(),
        cost_estimate=pl.CostEstimate(
            flops=heads * 8 * rows * rows * HEAD,
            bytes_accessed=heads * rows * (16 * HEAD + 2 * rows),
            transcendentals=0,
        ),
    )(owned, owned, owned, attended, grad_owned, weights)


def unpack_kernel(dest_ref, blocks_ref, q_ref, k_ref, v_ref, select):
    @pl.when(pl.program_id(0) == 0)
    def _():
        select[...] = as_bf16(dest_ref[:, 0:1] == lax.broadcasted_iota(jnp.int32, select.shape, 1))

    picked = dot32(select[...], blocks_ref[...]).astype(jnp.bfloat16)
    q_ref[...] = picked[:, 0:HEAD]
    k_ref[...] = picked[:, HEAD : 2 * HEAD]
    v_ref[...] = picked[:, 2 * HEAD :]


def unpack_grads(dest_col, blocks, heads):
    rows = dest_col.shape[0]
    buffer_rows = blocks.shape[0]
    out = jax.ShapeDtypeStruct((rows, heads * HEAD), jnp.bfloat16)
    return pl.pallas_call(
        unpack_kernel,
        grid=(heads,),
        in_specs=[
            pl.BlockSpec((rows, HEAD), lambda h: (0, 0)),
            pl.BlockSpec((buffer_rows, 3 * HEAD), lambda h: (0, h)),
        ],
        out_specs=[pl.BlockSpec((rows, HEAD), lambda h: (0, h))] * 3,
        out_shape=(out, out, out),
        scratch_shapes=[pltpu.VMEM((rows, buffer_rows), jnp.bfloat16)],
        compiler_params=params(),
        cost_estimate=pl.CostEstimate(
            flops=6 * heads * rows * buffer_rows * HEAD,
            bytes_accessed=6 * heads * HEAD * (rows + buffer_rows),
            transcendentals=0,
        ),
    )(dest_col, blocks)


def exchange(matrix, seq_count):
    rows, cols = matrix.shape
    blocks = matrix.reshape(seq_count, rows // seq_count, cols)
    return lax.all_to_all(blocks, "seq", split_axis=0, concat_axis=0, tiled=True).reshape(rows, cols)


def body(queries, key_rows, values, out_weight, grad_out, labels, owner_map, pair_mask):
    seq_count = lax.axis_size("seq")
    row_count, width = queries.shape
    heads = width // HEAD
    slot_size = 2 * row_count // seq_count
    buffer_rows = seq_count * slot_size
    scale = HEAD ** (-0.5)
    weight_t = lax.all_gather(out_weight.T, "seq", axis=0, tiled=True)
    near, far, order = gather_groups(grad_out)
    packed, dest_row, dest_col, code_row = pack_inputs(
        seq_count, slot_size, labels, owner_map, queries, key_rows, values
    )
    owned = exchange(packed, seq_count)
    code_row, near = lax.optimization_barrier((code_row, near))
    codes = gather_codes(code_row, slot_size)
    attended, weights = attention_forward(owned, codes, pair_mask.astype(jnp.bfloat16), heads, scale)
    returned = exchange(attended, seq_count)
    grad_owned = exchange(project_grads(order, near, far, weight_t, dest_row, buffer_rows), seq_count)
    partial_out = project_output(dest_col, returned, weight_t, lax.axis_size("tp"))
    output = lax.psum_scatter(partial_out, "tp", scatter_dimension=0, tiled=False)
    grads = attention_backward(owned, attended, grad_owned, weights, heads, scale)
    back = exchange(grads, seq_count)
    grad_q, grad_k, grad_v = unpack_grads(dest_col, back, heads)
    return (output, grad_q, grad_k, grad_v)


def solution(mesh):
    in_specs = (
        P("seq", "tp"),
        P("seq", "tp"),
        P("seq", "tp"),
        P("tp", "seq"),
        P("seq", "tp"),
        P("seq"),
        P(),
        P(),
    )
    out_specs = (P("seq", "tp"), P("seq", "tp"), P("seq", "tp"), P("seq", "tp"))
    return jax.shard_map(body, mesh=mesh, in_specs=in_specs, out_specs=out_specs, check_vma=False)
```

```python
import jax
import jax.numpy as jnp
from jax import lax
from jax.experimental import pallas as pl
from jax.experimental.pallas import tpu as pltpu
from jax.sharding import PartitionSpec as P

HEAD = 128
NEG_FILL = -1e30
LOG2_E = 1.4426950408889634
Y_COUNT = 4
Z_COUNT = 8
VMEM_BYTES = 48 * 1024 * 1024
VMEM_WHOLE = 60 * 1024 * 1024
NT = (((1,), (1,)), ((), ()))


def dot32(left, right):
    return jnp.dot(left, right, preferred_element_type=jnp.float32)


def dot32_nt(left, right):
    return lax.dot_general(left, right, NT, preferred_element_type=jnp.float32)


def params(limit=VMEM_BYTES):
    return pltpu.CompilerParams(vmem_limit_bytes=limit)


def as_bf16(flags):
    return flags.astype(jnp.float32).astype(jnp.bfloat16)


def column_of(row):
    wide = jnp.broadcast_to(row.astype(jnp.float32), (HEAD, row.shape[1]))
    return jnp.transpose(wide)


def pack_kernel(
    seq_count, slot_size, label_row, owner_row_ref, q_ref, k_ref, v_ref, packed, dest_row, dest_col, code_row, held, parts, in_sems, out_sems
):
    sources = (q_ref, k_ref, v_ref)
    rows, cols = q_ref.shape
    clusters = owner_row_ref.shape[1]
    buffer_rows = packed.shape[0]
    loads = [pltpu.make_async_copy(ref, held.at[i], in_sems.at[i]) for i, ref in enumerate(sources)]
    for load in loads:
        load.start()
    labels = label_row[...].reshape(1, rows)
    owner_col = column_of(owner_row_ref[...])[:, 0:1].astype(jnp.int32)
    in_cluster = labels == lax.broadcasted_iota(jnp.int32, (clusters, rows), 0)
    owner_row = jnp.sum(jnp.where(in_cluster, owner_col, 0), axis=0, keepdims=True)
    owned = owner_row == lax.broadcasted_iota(jnp.int32, (seq_count, rows), 0)
    earlier = lax.broadcasted_iota(jnp.int32, (rows, rows), 0) < lax.broadcasted_iota(
        jnp.int32, (rows, rows), 1
    )
    before = dot32(as_bf16(owned), as_bf16(earlier))
    rank_row = jnp.sum(jnp.where(owned, before, 0.0), axis=0, keepdims=True)
    dest = owner_row * slot_size + rank_row.astype(jnp.int32)
    dest_row[...] = dest
    select = as_bf16(lax.broadcasted_iota(jnp.int32, (buffer_rows, rows), 0) == dest)
    stores = []

    def store(start, stop):
        part = slice(start, stop)
        stores.append(pltpu.make_async_copy(parts.at[:, part], packed.at[:, part], out_sems.at[len(stores)]))
        stores[-1].start()

    for i, load in enumerate(loads):
        load.wait()
        parts[:, i * cols : (i + 1) * cols] = dot32(select, held[i]).astype(jnp.bfloat16)
        store(i * cols, (i + 1) * cols)
    codes = jnp.broadcast_to((labels + 1).astype(jnp.float32), (16, rows)).astype(jnp.bfloat16)
    code_row[...] = dot32_nt(codes, select)[0:1].astype(jnp.int32)
    dest_col[...] = column_of(dest).astype(jnp.int32)
    for copy in stores:
        copy.wait()


def pack_inputs(seq_count, slot_size, labels, owner_map, queries, key_rows, values):
    rows, cols = queries.shape
    buffer_rows = seq_count * slot_size
    return pl.pallas_call(
        lambda *refs: pack_kernel(seq_count, slot_size, *refs),
        out_shape=(
            jax.ShapeDtypeStruct((buffer_rows, 3 * cols), jnp.bfloat16),
            jax.ShapeDtypeStruct((1, rows), jnp.int32),
            jax.ShapeDtypeStruct((rows, HEAD), jnp.int32),
            jax.ShapeDtypeStruct((1, buffer_rows), jnp.int32),
        ),
        in_specs=[pl.BlockSpec(memory_space=pltpu.VMEM)] * 2 + [pl.BlockSpec(memory_space=pl.ANY)] * 3,
        out_specs=(pl.BlockSpec(memory_space=pl.ANY),) + (pl.BlockSpec(memory_space=pltpu.VMEM),) * 3,
        scratch_shapes=[
            pltpu.VMEM((3, rows, cols), jnp.bfloat16),
            pltpu.VMEM((buffer_rows, 3 * cols), jnp.bfloat16),
            pltpu.SemaphoreType.DMA((3,)),
            pltpu.SemaphoreType.DMA((3,)),
        ],
        compiler_params=params(VMEM_WHOLE),
    )(labels, owner_map[None, :], queries, key_rows, values)


def grad_kernel(order_ref, near_ref, far_ref, weight_ref, dest_row, packed, total):
    step = pl.program_id(0)
    half = pl.num_programs(0) // 2

    @pl.when(step == 0)
    def _():
        total[...] = jnp.zeros_like(total)

    @pl.when(step < half)
    def _():
        total[...] += dot32(near_ref[0], weight_ref[...])

    @pl.when(step >= half)
    def _():
        total[...] += dot32(far_ref[0], weight_ref[...])

    @pl.when(step == pl.num_programs(0) - 1)
    def _():
        select = as_bf16(lax.broadcasted_iota(jnp.int32, (packed.shape[0], total.shape[0]), 0) == dest_row[...])
        packed[...] = dot32(select, total[...].astype(jnp.bfloat16)).astype(jnp.bfloat16)


def project_grads(order, near, far, weight_t, dest_row, buffer_rows):
    half, rows, width = near.shape
    groups = 2 * half
    return pl.pallas_call(
        grad_kernel,
        grid_spec=pltpu.PrefetchScalarGridSpec(
            num_scalar_prefetch=1,
            grid=(groups,),
            in_specs=[
                pl.BlockSpec((1, rows, width), lambda g, order: (jnp.minimum(g, half - 1), 0, 0)),
                pl.BlockSpec((1, rows, width), lambda g, order: (jnp.maximum(g - half, 0), 0, 0)),
                pl.BlockSpec((width, width), lambda g, order: (order[g], 0)),
                pl.BlockSpec((1, rows), lambda g, order: (0, 0)),
            ],
            out_specs=pl.BlockSpec((buffer_rows, width), lambda g, order: (0, 0)),
            scratch_shapes=[pltpu.VMEM((rows, width), jnp.float32)],
        ),
        out_shape=jax.ShapeDtypeStruct((buffer_rows, width), jnp.bfloat16),
        compiler_params=params(VMEM_WHOLE),
        cost_estimate=pl.CostEstimate(
            flops=2 * groups * rows * width * width + 2 * buffer_rows * rows * width,
            bytes_accessed=2 * groups * width * (rows + width),
            transcendentals=0,
        ),
    )(order, near, far, weight_t, dest_row)


def output_kernel(dest_col, returned, weight_ref, out_ref, local):
    @pl.when(pl.program_id(0) == 0)
    def _():
        place = lax.broadcasted_iota(jnp.int32, (local.shape[0], returned.shape[0]), 1)
        local[...] = dot32(as_bf16(dest_col[:, 0:1] == place), returned[...]).astype(jnp.bfloat16)

    out_ref[0] = dot32_nt(local[...], weight_ref[...]).astype(jnp.bfloat16)


def project_output(dest_col, returned, weight_t, groups):
    rows = dest_col.shape[0]
    buffer_rows, width = returned.shape
    return pl.pallas_call(
        output_kernel,
        grid=(groups,),
        in_specs=[
            pl.BlockSpec((rows, HEAD), lambda g: (0, 0)),
            pl.BlockSpec((buffer_rows, width), lambda g: (0, 0)),
            pl.BlockSpec((width, width), lambda g: (g, 0)),
        ],
        out_specs=pl.BlockSpec((1, rows, width), lambda g: (g, 0, 0)),
        out_shape=jax.ShapeDtypeStruct((groups, rows, width), jnp.bfloat16),
        scratch_shapes=[pltpu.VMEM((rows, width), jnp.bfloat16)],
        compiler_params=params(),
        cost_estimate=pl.CostEstimate(
            flops=2 * groups * rows * width * width + 2 * buffer_rows * rows * width,
            bytes_accessed=2 * groups * width * (rows + width),
            transcendentals=0,
        ),
    )(dest_col, returned, weight_t)


def gather_groups(block):
    tp_count = lax.axis_size("tp")
    half = tp_count // 2
    near = [block]
    for shift in range(1, half):
        near.append(lax.ppermute(block, "tp", [(t, (t + 2 * shift) % tp_count) for t in range(tp_count)]))
    near = jnp.stack(near)
    far = lax.ppermute(near, "tp", [(t, t ^ 1) for t in range(tp_count)])
    me = lax.axis_index("tp")
    own = (me + tp_count - 2 * jnp.arange(half, dtype=jnp.int32)) % tp_count
    return near, far, jnp.concatenate([own, own ^ 1])


def gather_codes(code_row, slot_size):
    def move(block, along_y, along_z):
        steps = [
            (y * Z_COUNT + z, (y + along_y) % Y_COUNT * Z_COUNT + (z + along_z) % Z_COUNT)
            for y in range(Y_COUNT)
            for z in range(Z_COUNT)
        ]
        return lax.ppermute(block, "seq", steps)

    rows = jnp.concatenate([code_row] + [move(code_row, turn, 0) for turn in range(1, Y_COUNT)])
    table = jnp.concatenate([rows] + [move(rows, 0, turn) for turn in range(1, Z_COUNT)])
    me = lax.axis_index("seq")
    mine = lax.dynamic_slice_in_dim(table, me * slot_size, slot_size, 1)
    source = jnp.arange(Y_COUNT * Z_COUNT, dtype=jnp.int32)
    turn_y = (me // Z_COUNT - source // Z_COUNT + Y_COUNT) % Y_COUNT
    turn_z = (me - source + Y_COUNT * Z_COUNT) % Z_COUNT
    codes = mine[turn_z * Y_COUNT + turn_y].reshape(-1, 1)
    return jnp.broadcast_to(codes, (codes.shape[0], HEAD)).astype(jnp.bfloat16)


def forward_kernel(scale, q_ref, k_ref, v_ref, code_ref, mask_ref, att_ref, weight_ref, keys, asks):
    rows = q_ref.shape[0]

    @pl.when(pl.program_id(0) == 0)
    def _():
        lane = lax.broadcasted_iota(jnp.int32, (rows, HEAD), 1).astype(jnp.float32) + 1.0
        code = code_ref[...].astype(jnp.float32)
        onehot = as_bf16((code == lane) | (code == 0.0))
        linked = dot32(onehot, mask_ref[...])
        keys[:, HEAD:] = onehot
        asks[:, HEAD:] = jnp.where(linked > 0.5, 0.0, NEG_FILL).astype(jnp.bfloat16)

    keys[:, :HEAD] = k_ref[...]
    asks[:, :HEAD] = q_ref[...]
    scores = dot32_nt(keys[...], asks[...])
    top = jnp.max(scores, axis=0, keepdims=True)
    terms = jnp.exp2((scores - top) * (scale * LOG2_E))
    weights = (terms * (1.0 / jnp.sum(terms, axis=0, keepdims=True))).astype(jnp.bfloat16)
    weight_ref[0] = weights
    att_ref[...] = jnp.transpose(dot32(jnp.transpose(v_ref[...]), weights)).astype(jnp.bfloat16)


def backward_kernel(scale, q_ref, k_ref, v_ref, att_ref, g_ref, weight_ref, out_ref):
    grad = g_ref[...]
    weights = weight_ref[0]
    delta = jnp.sum(
        jnp.transpose(grad.astype(jnp.float32) * att_ref[...].astype(jnp.float32)), axis=0, keepdims=True
    )
    grad_probs = dot32_nt(v_ref[...], grad)
    grad_scores = (weights.astype(jnp.float32) * (grad_probs - delta)).astype(jnp.bfloat16)
    grad_query = dot32(jnp.transpose(k_ref[...]), grad_scores) * scale
    out_ref[:, 0:HEAD] = jnp.transpose(grad_query).astype(jnp.bfloat16)
    out_ref[:, HEAD : 2 * HEAD] = (dot32(grad_scores, q_ref[...]) * scale).astype(jnp.bfloat16)
    out_ref[:, 2 * HEAD :] = dot32(weights, grad).astype(jnp.bfloat16)


def attention_forward(owned, codes, pair_mask, heads, scale):
    rows = owned.shape[0]
    block = (rows, HEAD)
    return pl.pallas_call(
        lambda *refs: forward_kernel(scale, *refs),
        grid=(heads,),
        in_specs=[
            pl.BlockSpec(block, lambda h: (0, h)),
            pl.BlockSpec(block, lambda h: (0, heads + h)),
            pl.BlockSpec(block, lambda h: (0, 2 * heads + h)),
            pl.BlockSpec(block, lambda h: (0, 0)),
            pl.BlockSpec(pair_mask.shape, lambda h: (0, 0)),
        ],
        out_specs=(
            pl.BlockSpec(block, lambda h: (0, h)),
            pl.BlockSpec((1, rows, rows), lambda h: (h, 0, 0)),
        ),
        out_shape=(
            jax.ShapeDtypeStruct((rows, heads * HEAD), jnp.bfloat16),
            jax.ShapeDtypeStruct((heads, rows, rows), jnp.bfloat16),
        ),
        scratch_shapes=[pltpu.VMEM((rows, 2 * HEAD), jnp.bfloat16)] * 2,
        compiler_params=params(),
        cost_estimate=pl.CostEstimate(
            flops=heads * 4 * rows * rows * HEAD,
            bytes_accessed=heads * rows * (8 * HEAD + 2 * rows),
            transcendentals=heads * rows * rows,
        ),
    )(owned, owned, owned, codes, pair_mask)


def attention_backward(owned, attended, grad_owned, weights, heads, scale):
    rows = owned.shape[0]
    block = (rows, HEAD)
    return pl.pallas_call(
        lambda *refs: backward_kernel(scale, *refs),
        grid=(heads,),
        in_specs=[
            pl.BlockSpec(block, lambda h: (0, h)),
            pl.BlockSpec(block, lambda h: (0, heads + h)),
            pl.BlockSpec(block, lambda h: (0, 2 * heads + h)),
            pl.BlockSpec(block, lambda h: (0, h)),
            pl.BlockSpec(block, lambda h: (0, h)),
            pl.BlockSpec((1, rows, rows), lambda h: (h, 0, 0)),
        ],
        out_specs=pl.BlockSpec((rows, 3 * HEAD), lambda h: (0, h)),
        out_shape=jax.ShapeDtypeStruct((rows, 3 * heads * HEAD), jnp.bfloat16),
        compiler_params=params(),
        cost_estimate=pl.CostEstimate(
            flops=heads * 8 * rows * rows * HEAD,
            bytes_accessed=heads * rows * (16 * HEAD + 2 * rows),
            transcendentals=0,
        ),
    )(owned, owned, owned, attended, grad_owned, weights)


def unpack_kernel(heads, dest_ref, blocks_ref, *refs):
    outs, (held, sems) = refs[:3], refs[3:]
    rows = dest_ref.shape[0]
    select = as_bf16(dest_ref[:, 0:1] == lax.broadcasted_iota(jnp.int32, (rows, blocks_ref.shape[0]), 1))
    copies = []
    for head in range(heads):
        wide = slice(head * 3 * HEAD, (head + 1) * 3 * HEAD)
        held[:, wide] = dot32(select, blocks_ref[:, wide]).astype(jnp.bfloat16)
        for place, out_ref in enumerate(outs):
            start = (head * 3 + place) * HEAD
            source = held.at[:, start : start + HEAD]
            target = out_ref.at[:, head * HEAD : (head + 1) * HEAD]
            copies.append(pltpu.make_async_copy(source, target, sems.at[head * 3 + place]))
            copies[-1].start()
    for copy in copies:
        copy.wait()


def unpack_grads(dest_col, blocks, heads):
    rows = dest_col.shape[0]
    buffer_rows, cols = blocks.shape
    out = jax.ShapeDtypeStruct((rows, heads * HEAD), jnp.bfloat16)
    return pl.pallas_call(
        lambda *refs: unpack_kernel(heads, *refs),
        in_specs=[pl.BlockSpec(memory_space=pltpu.VMEM)] * 2,
        out_specs=(pl.BlockSpec(memory_space=pl.ANY),) * 3,
        out_shape=(out, out, out),
        scratch_shapes=[pltpu.VMEM((rows, cols), jnp.bfloat16), pltpu.SemaphoreType.DMA((3 * heads,))],
        compiler_params=params(),
        cost_estimate=pl.CostEstimate(
            flops=6 * heads * rows * buffer_rows * HEAD,
            bytes_accessed=6 * heads * HEAD * (rows + buffer_rows),
            transcendentals=0,
        ),
    )(dest_col, blocks)


def exchange(matrix, seq_count):
    rows, cols = matrix.shape
    blocks = matrix.reshape(seq_count, rows // seq_count, cols)
    return lax.all_to_all(blocks, "seq", split_axis=0, concat_axis=0, tiled=True).reshape(rows, cols)


def body(queries, key_rows, values, out_weight, grad_out, labels, owner_map, pair_mask):
    seq_count = lax.axis_size("seq")
    row_count, width = queries.shape
    heads = width // HEAD
    slot_size = 2 * row_count // seq_count
    buffer_rows = seq_count * slot_size
    scale = HEAD ** (-0.5)
    weight_t = lax.all_gather(out_weight.T, "seq", axis=0, tiled=True)
    near, far, order = gather_groups(grad_out)
    packed, dest_row, dest_col, code_row = pack_inputs(
        seq_count, slot_size, labels, owner_map, queries, key_rows, values
    )
    owned = exchange(packed, seq_count)
    code_row, near = lax.optimization_barrier((code_row, near))
    codes = gather_codes(code_row, slot_size)
    attended, weights = attention_forward(owned, codes, pair_mask.astype(jnp.bfloat16), heads, scale)
    returned = exchange(attended, seq_count)
    grad_owned = exchange(project_grads(order, near, far, weight_t, dest_row, buffer_rows), seq_count)
    partial_out = project_output(dest_col, returned, weight_t, lax.axis_size("tp"))
    output = lax.psum_scatter(partial_out, "tp", scatter_dimension=0, tiled=False)
    grads = attention_backward(owned, attended, grad_owned, weights, heads, scale)
    back = exchange(grads, seq_count)
    grad_q, grad_k, grad_v = unpack_grads(dest_col, back, heads)
    return (output, grad_q, grad_k, grad_v)


def solution(mesh):
    in_specs = (
        P("seq", "tp"),
        P("seq", "tp"),
        P("seq", "tp"),
        P("tp", "seq"),
        P("seq", "tp"),
        P("seq"),
        P(),
        P(),
    )
    out_specs = (P("seq", "tp"), P("seq", "tp"), P("seq", "tp"), P("seq", "tp"))
    return jax.shard_map(body, mesh=mesh, in_specs=in_specs, out_specs=out_specs, check_vma=False)
```
